512 devices in a mesh: grp: 16 (over x, y_lo, core), loop: 32 (over y_hi, z).
Axes of the slice: x: 4, y: 4 (y_hi: 2, y_lo: 2; y = y_hi * 2 + y_lo), z: 16, core: 2. Of those that a mesh axis runs over, the one named last changes fastest.
Arguments:
- vision_tower_output: bfloat16 [32768, 1536], P(('grp', 'loop')), may hold values from -0.1796875 to 0.1796875
- language_tower_output: bfloat16 [32768, 1536], P(('grp', 'loop')), may hold values from -0.1796875 to 0.1796875
- sharpness_factor: float32 [1], replicated, may hold values from 4 to 16
- shift_added: float32 [1], replicated, may hold values from -3 to -1
Outputs:
- image_gradient: float32 [32768, 1536], P(('grp', 'loop'))
- grad_texts: float32 [32768, 1536], P(('grp', 'loop'))
The draws below stay inside these ranges and needn't reach their ends.
All inputs are finite; a program needn't handle non-finite values.
Results may differ from the reference program's by a relative error of at most 0.023.
Values may be sent and summed in bfloat16 or wider, within the bound.
A program may use at most 128 MiB of HBM per device.

```python
import math
import jax
import jax.numpy as jnp
from jax import lax

E = 1536
B_DEV = 64
HOPS = 4
BATCH = 32768
N_GRP = 16
N_LOOP = 32


def levels(key, dims, pieces, least, high):
    def one(axis_at, blocks):
        steps = jax.random.uniform(jax.random.fold_in(jax.random.fold_in(key, 6), axis_at), (blocks,), jnp.float32, least / len(pieces), high / len(pieces))
        return jnp.repeat(jnp.exp(steps), dims[axis_at] // blocks).reshape((-1,) + (1,) * (len(dims) - axis_at - 1))

    level = one(*pieces[0])
    for cut in pieces[1:]:
        level = level * one(*cut)
    return level


def normal_values(rng, shape, width, most, cuts=(), held_as=jnp.bfloat16):
    values = width * jax.random.normal(rng, shape, jnp.float32)
    if cuts:
        values = values * levels(rng, shape, cuts, -0.22, 0.18)
    return jnp.clip(values, -most, most).astype(held_as)


def setup_inputs(seed: int = 0) -> dict:
    splits = jax.random.split(jax.random.key(seed), 5)
    return {
        "vision_tower_output": normal_values(splits[0], (BATCH, E), 0.03, 0.1796875, ((0, 512),)),
        "language_tower_output": normal_values(splits[1], (BATCH, E), 0.03, 0.1796875, ((0, 512),)),
        "sharpness_factor": jnp.clip(jnp.exp(jax.random.uniform(splits[2], (1,), jnp.float32, math.log(4.0), math.log(16.0))), 4.0, 16.0),
        "shift_added": jnp.clip(jax.random.uniform(splits[3], (1,), jnp.float32, -3.0, -1.0), -3.0, -1.0),
    }


def normalize_each_entry_line(values):
    wide = values.astype(jnp.float32)
    inverse = lax.rsqrt(lax.optimization_barrier(jnp.sum(wide * wide, axis=-1, keepdims=True)) + 1e-06)
    return (wide * inverse, inverse)

def coefficient_block(picture_rows, txt_rows, similarity_multiplier, group_offset, positive):
    score = jnp.einsum('ie,je->ij', picture_rows.astype(jnp.float32), txt_rows.astype(jnp.float32)) * similarity_multiplier + group_offset
    sign = jnp.where(positive, 1.0, -1.0).astype(jnp.float32)
    return (-sign * jax.nn.sigmoid(-sign * score) * similarity_multiplier).astype(jnp.bfloat16)

def back_norm(unit, inverse, grad):
    return (grad - unit * lax.optimization_barrier(jnp.sum(unit * grad, axis=-1, keepdims=True))) * inverse

def reference(vision_tower_output, language_tower_output, sharpness_factor, shift_added):
    group = N_GRP * B_DEV
    similarity_multiplier = sharpness_factor[0]
    group_offset = shift_added[0]
    unit_img, inv_img = normalize_each_entry_line(vision_tower_output)
    unit_txt, reciprocal_textual_norm = normalize_each_entry_line(language_tower_output)
    visual_embedding_vectors = unit_img.astype(jnp.bfloat16)
    emb_txt = unit_txt.astype(jnp.bfloat16)

    def arrange_groups(values):
        return values.reshape(N_GRP, N_LOOP, B_DEV, E).transpose(1, 0, 2, 3).reshape(N_LOOP, group, E)

    def restore(values):
        return values.reshape(N_LOOP, N_GRP, B_DEV, E).transpose(1, 0, 2, 3).reshape(N_GRP * N_LOOP * B_DEV, E)
    img_three = arrange_groups(visual_embedding_vectors)
    txt_three = arrange_groups(emb_txt)
    diagonal = jnp.arange(group)[:, None] == jnp.arange(group)[None, :]
    loops = jnp.arange(N_LOOP).astype(jnp.int32)

    def image_side(place):
        picture_rows = lax.dynamic_index_in_dim(img_three, place, 0, keepdims=False)
        total = jnp.zeros((group, E), jnp.float32)
        for step in range(HOPS + 1):
            other = ((place - step) % N_LOOP).astype(jnp.int32)
            txt_rows = lax.dynamic_index_in_dim(txt_three, other, 0, keepdims=False)
            coef = coefficient_block(picture_rows, txt_rows, similarity_multiplier, group_offset, diagonal if step == 0 else False)
            total = total + jnp.einsum('ij,je->ie', coef.astype(jnp.float32), txt_rows.astype(jnp.float32))
        return total

    def text_side(place):
        txt_rows = lax.dynamic_index_in_dim(txt_three, place, 0, keepdims=False)
        partial_value = jnp.zeros((N_GRP, group, E), jnp.float32)
        for step in range(HOPS + 1):
            other = ((place + step) % N_LOOP).astype(jnp.int32)
            picture_rows = lax.dynamic_index_in_dim(img_three, other, 0, keepdims=False)
            coef = coefficient_block(picture_rows, txt_rows, similarity_multiplier, group_offset, diagonal if step == 0 else False)
            partial_value = partial_value + jnp.einsum('grj,gre->gje', coef.reshape(N_GRP, B_DEV, group).astype(jnp.float32), picture_rows.reshape(N_GRP, B_DEV, E).astype(jnp.float32))
        rounded = lax.optimization_barrier(partial_value.astype(jnp.bfloat16))
        return lax.optimization_barrier(jnp.sum(rounded.astype(jnp.float32), axis=0))
    grad_emb_img = restore(lax.map(image_side, loops))
    grad_emb_txt = restore(lax.map(text_side, loops))
    return (back_norm(unit_img, inv_img, grad_emb_img), back_norm(unit_txt, reciprocal_textual_norm, grad_emb_txt))
```

```python
import functools

import jax
import jax.numpy as jnp
from jax import lax
from jax.experimental import pallas as pl
from jax.experimental.pallas import tpu as pltpu
from jax.sharding import PartitionSpec as P

HOPS = 4
ROWS = 64
HALF = 32
WIDE = 1536
XS = 4
MESH = pl.DeviceIdType.MESH
F32 = jnp.float32
BF16 = jnp.bfloat16


def half(c):
    return pl.ds(c * HALF, HALF)


def inverse_norm(ref):
    wide = ref[...].astype(F32)
    return lax.rsqrt(jnp.sum(wide * wide, axis=-1, keepdims=True) + 1e-06)


def back_norm(raw_ref, inverse, grad):
    unit = raw_ref[...].astype(F32) * inverse
    return (grad - unit * jnp.sum(unit * grad, axis=-1, keepdims=True)) * inverse


def kernel(
    loops,
    factor_ref,
    shift_ref,
    img_ref,
    txt_ref,
    img_out,
    txt_out,
    imgs,
    txts,
    coefs,
    grads,
    text_sum,
    other_out,
    other_in,
    chain_out,
    chain_in,
    part_out,
    first_a,
    first_b,
    second,
    row_out,
    row_in,
    send_sem,
    recv_sem,
):
    g = lax.axis_index("grp")
    q = lax.axis_index("loop")
    x = g // 4
    y = (g // 2) % 2
    core = g % 2

    def member(xx, yy, cc):
        return {"grp": xx * 4 + yy * 2 + cc, "loop": q}

    twin = member(x, y, 1 - core)
    across = member(x, 1 - y, core)
    right = member((x + 1) % XS, y, core)
    left = member((x + XS - 1) % XS, y, core)
    below = {"grp": g, "loop": (q + loops - 1) % loops}
    above = {"grp": g, "loop": (q + 1) % loops}

    barrier = pltpu.get_barrier_semaphore()
    peers = (twin, across, right, left, below, above)
    for peer in peers:
        pl.semaphore_signal(barrier, inc=1, device_id=peer, device_id_type=MESH)

    copies = []

    def link(src, dst, device):
        i = len(copies)
        copy = pltpu.make_async_remote_copy(
            src_ref=src,
            dst_ref=dst,
            send_sem=send_sem.at[i],
            recv_sem=recv_sem.at[i],
            device_id=device,
            device_id_type=MESH,
        )
        copies.append(copy)
        return copy

    down = {
        (h, c): link(imgs.at[h - 1, 0, half(c)], imgs.at[h, 0, half(c)], below)
        for h in range(1, HOPS + 1)
        for c in range(2)
    }
    to_twin = {
        (h, c): link(imgs.at[h, 0, half(c)], imgs.at[h, 1, half(c)], twin)
        for h in range(HOPS + 1)
        for c in range(2)
    }
    text_y = [link(txts.at[0, 0, half(c)], txts.at[1, 0, half(c)], across) for c in range(2)]
    text_right = {
        (r, c): link(txts.at[r, 0, half(c)], txts.at[r, 3, half(c)], right)
        for r in range(2)
        for c in range(2)
    }
    text_left = {
        (r, c): link(txts.at[r, 0, half(c)], txts.at[r, 1, half(c)], left)
        for r in range(2)
        for c in range(2)
    }
    text_far_a = [link(txts.at[r, 3, half(0)], txts.at[r, 2, half(0)], right) for r in range(2)]
    text_far_b = [link(txts.at[r, 1, half(1)], txts.at[r, 2, half(1)], left) for r in range(2)]
    term = {
        (h, c): link(other_out.at[h, half(c)], other_in.at[h, half(c)], twin)
        for h in range(HOPS + 1)
        for c in range(2)
    }
    up = {
        (h, c): link(chain_out.at[h - 1, half(c)], chain_in.at[h - 1, half(c)], above)
        for h in range(1, HOPS + 1)
        for c in range(2)
    }
    far_a = [link(part_out.at[r, 2, half(0)], first_a.at[r], right) for r in range(2)]
    far_b = [link(part_out.at[r, 2, half(1)], first_b.at[r], left) for r in range(2)]
    near_right = {
        (r, c): link(part_out.at[r, 1, half(c)], second.at[r, 0, half(c)], right)
        for r in range(2)
        for c in range(2)
    }
    near_left = {
        (r, c): link(part_out.at[r, 3, half(c)], second.at[r, 1, half(c)], left)
        for r in range(2)
        for c in range(2)
    }
    over = [link(row_out.at[half(c)], row_in.at[half(c)], across) for c in range(2)]

    factor = factor_ref[0]
    shift = shift_ref[0]

    inv_img = inverse_norm(img_ref)
    imgs[0, 0] = (img_ref[...].astype(F32) * inv_img).astype(BF16)
    inv_txt = inverse_norm(txt_ref)
    txts[0, 0] = (txt_ref[...].astype(F32) * inv_txt).astype(BF16)

    pl.semaphore_wait(barrier, len(peers))

    for c in range(2):
        down[1, c].start()
        text_y[c].start()
        text_right[0, c].start()
        text_left[0, c].start()
        to_twin[0, c].start()

    def pass_on(h, c):
        down[h, c].wait_recv()
        if h < HOPS:
            down[h + 1, c].start()
        to_twin[h, c].start()

    def score(h, r):
        pictures = imgs[h].reshape(2 * ROWS, WIDE)
        words = txts[r].reshape(XS * ROWS, WIDE)
        s = lax.dot_general(
            pictures, words, (((1,), (1,)), ((), ())), preferred_element_type=F32
        )
        s = s * factor + shift
        if h == 0 and r == 0:
            rows = lax.broadcasted_iota(jnp.int32, s.shape, 0)
            cols = lax.broadcasted_iota(jnp.int32, s.shape, 1)
            positive = (rows == cols) & (rows < ROWS)
            sign = jnp.where(positive, 1.0, -1.0).astype(F32)
            value = -sign * jax.nn.sigmoid(-sign * s) * factor
        else:
            value = jax.nn.sigmoid(s) * factor
        coefs[h, :, r * XS * ROWS : (r + 1) * XS * ROWS] = value.astype(BF16)

    def image_terms(h):
        words = txts[...].reshape(2 * XS * ROWS, WIDE)
        out = jnp.dot(coefs[h], words, preferred_element_type=F32)
        grads[h] = out[:ROWS]
        other_out[h] = out[ROWS:].astype(BF16)
        for c in range(2):
            term[h, c].start()

    def climb(h, c):
        term[h, c].wait_recv()
        total = grads[h, half(c)] + other_in[h, half(c)].astype(F32)
        if h < HOPS:
            up[h + 1, c].wait_recv()
            total = total + chain_in[h, half(c)].astype(F32)
        if h > 0:
            chain_out[h - 1, half(c)] = total.astype(BF16)
            up[h, c].start()
        else:
            grads[0, half(c)] = total

    pass_on(1, 0)
    text_y[0].wait_recv()
    text_right[1, 0].start()
    text_left[1, 0].start()
    pass_on(1, 1)
    text_y[1].wait_recv()
    text_right[1, 1].start()
    text_left[1, 1].start()
    text_right[0, 0].wait_recv()
    text_far_a[0].start()
    text_left[0, 1].wait_recv()
    text_far_b[0].start()
    pass_on(2, 0)
    text_right[1, 0].wait_recv()
    text_far_a[1].start()
    pass_on(2, 1)
    text_left[1, 1].wait_recv()
    text_far_b[1].start()
    text_right[0, 1].wait_recv()
    text_left[0, 0].wait_recv()
    text_far_a[0].wait_recv()
    text_far_b[0].wait_recv()
    for c in range(2):
        to_twin[0, c].wait_recv()
    score(0, 0)
    pass_on(3, 0)
    for c in range(2):
        to_twin[1, c].wait_recv()
    score(1, 0)
    for c in range(2):
        to_twin[2, c].wait_recv()
    score(2, 0)
    text_right[1, 1].wait_recv()
    text_left[1, 0].wait_recv()
    text_far_a[1].wait_recv()
    text_far_b[1].wait_recv()
    pass_on(3, 1)
    score(0, 1)
    score(1, 1)
    score(2, 1)
    image_terms(0)
    image_terms(1)
    pass_on(4, 0)
    image_terms(2)
    for c in range(2):
        to_twin[3, c].wait_recv()
    score(3, 0)
    score(3, 1)
    image_terms(3)
    pass_on(4, 1)
    early = coefs[0:HOPS].reshape(HOPS * 2 * ROWS, 2 * XS * ROWS)
    pictures = imgs[0:HOPS].reshape(HOPS * 2 * ROWS, WIDE)
    text_sum[...] = lax.dot_general(
        early, pictures, (((0,), (0,)), ((), ())), preferred_element_type=F32
    )
    for c in range(2):
        to_twin[4, c].wait_recv()
    score(4, 0)
    score(4, 1)
    image_terms(4)

    def text_part(r, k):
        at = (r * XS + k) * ROWS
        late = coefs[HOPS, :, at : at + ROWS]
        last = imgs[HOPS].reshape(2 * ROWS, WIDE)
        extra = lax.dot_general(
            late, last, (((0,), (0,)), ((), ())), preferred_element_type=F32
        )
        total = text_sum[at : at + ROWS] + extra
        text_sum[at : at + ROWS] = total
        part_out[r, k] = total.astype(BF16)

    for r in (1, 0):
        text_part(r, 2)
        far_a[r].start()
        far_b[r].start()
    climb(4, 0)
    climb(4, 1)

    for r in (1, 0):
        text_part(r, 1)
        near_right[r, 1].start()
        text_part(r, 3)
        near_left[r, 0].start()
    text_part(1, 0)
    text_part(0, 0)

    def join(r):
        far_a[r].wait_recv()
        at = (r * XS + 1) * ROWS
        part_out[r, 1, half(0)] = (text_sum[at : at + HALF] + first_a[r].astype(F32)).astype(BF16)
        near_right[r, 0].start()
        far_b[r].wait_recv()
        at = (r * XS + 3) * ROWS + HALF
        part_out[r, 3, half(1)] = (text_sum[at : at + HALF] + first_b[r].astype(F32)).astype(BF16)
        near_left[r, 1].start()

    def row_total(r, c):
        near_right[r, c].wait_recv()
        near_left[r, c].wait_recv()
        at = r * XS * ROWS + c * HALF
        return (
            text_sum[at : at + HALF]
            + second[r, 0, half(c)].astype(F32)
            + second[r, 1, half(c)].astype(F32)
        )

    join(1)
    climb(3, 0)
    climb(3, 1)
    join(0)
    climb(2, 0)
    climb(2, 1)
    for c in range(2):
        row_out[half(c)] = row_total(1, c).astype(BF16)
        over[c].start()
    climb(1, 0)
    climb(1, 1)
    for c in range(2):
        text_sum[c * HALF : (c + 1) * HALF] = row_total(0, c)
    for c in range(2):
        over[c].wait_recv()
    txt_out[...] = back_norm(txt_ref, inv_txt, text_sum[0:ROWS] + row_in[...].astype(F32))
    climb(0, 0)
    climb(0, 1)
    img_out[...] = back_norm(img_ref, inv_img, grads[0])

    for copy in copies:
        copy.wait_send()


N_COPIES = 8 + 10 + 2 + 4 + 4 + 2 + 2 + 10 + 8 + 2 + 2 + 4 + 4 + 2


def per_device(loops, images, texts, factor, shift):
    vmem = pl.BlockSpec(memory_space=pltpu.VMEM)
    smem = pl.BlockSpec(memory_space=pltpu.SMEM)
    out = jax.ShapeDtypeStruct((ROWS, WIDE), F32)
    return pl.pallas_call(
        functools.partial(kernel, loops),
        out_shape=(out, out),
        in_specs=[smem, smem, vmem, vmem],
        out_specs=(vmem, vmem),
        scratch_shapes=[
            pltpu.VMEM((HOPS + 1, 2, ROWS, WIDE), BF16),
            pltpu.VMEM((2, XS, ROWS, WIDE), BF16),
            pltpu.VMEM((HOPS + 1, 2 * ROWS, 2 * XS * ROWS), BF16),
            pltpu.VMEM((HOPS + 1, ROWS, WIDE), F32),
            pltpu.VMEM((2 * XS * ROWS, WIDE), F32),
            pltpu.VMEM((HOPS + 1, ROWS, WIDE), BF16),
            pltpu.VMEM((HOPS + 1, ROWS, WIDE), BF16),
            pltpu.VMEM((HOPS, ROWS, WIDE), BF16),
            pltpu.VMEM((HOPS, ROWS, WIDE), BF16),
            pltpu.VMEM((2, XS, ROWS, WIDE), BF16),
            pltpu.VMEM((2, HALF, WIDE), BF16),
            pltpu.VMEM((2, HALF, WIDE), BF16),
            pltpu.VMEM((2, 2, ROWS, WIDE), BF16),
            pltpu.VMEM((ROWS, WIDE), BF16),
            pltpu.VMEM((ROWS, WIDE), BF16),
            pltpu.SemaphoreType.DMA((N_COPIES,)),
            pltpu.SemaphoreType.DMA((N_COPIES,)),
        ],
        compiler_params=pltpu.CompilerParams(
            collective_id=0, has_side_effects=True, vmem_limit_bytes=48 * 2**20
        ),
        name="siglip",
    )(factor, shift, images, texts)


def solution(mesh):
    loops = mesh.shape["loop"]
    spec = P(("grp", "loop"), None)

    def step(images, texts, factor, shift):
        return per_device(loops, images, texts, factor, shift)

    return jax.shard_map(
        step, mesh=mesh, in_specs=(spec, spec, P(), P()), out_specs=(spec, spec), check_vma=False
    )
```

```python
import functools

import jax
import jax.numpy as jnp
from jax import lax
from jax.experimental import pallas as pl
from jax.experimental.pallas import tpu as pltpu
from jax.sharding import PartitionSpec as P

HOPS = 4
ROWS = 64
HALF = 32
SLICE = 16
SLICES = ROWS // SLICE
WIDE = 1536
XS = 4
ZS = 16
MINE = XS * ROWS
WORDS = 2 * MINE
MESH = pl.DeviceIdType.MESH
F32 = jnp.float32
BF16 = jnp.bfloat16
BOTH_LAST = (((1,), (1,)), ((), ()))
BOTH_FIRST = (((0,), (0,)), ((), ()))


def half(c):
    return pl.ds(c * HALF, HALF)


def sliver(u):
    return pl.ds(u * SLICE, SLICE)


def inverse_norm(ref):
    wide = ref[...].astype(F32)
    return lax.rsqrt(jnp.sum(wide * wide, axis=-1, keepdims=True) + 1e-06)


def back_norm(raw, inverse, grad):
    unit = raw.astype(F32) * inverse
    return (grad - unit * jnp.sum(unit * grad, axis=-1, keepdims=True)) * inverse


def kernel(
    loops,
    factor_ref,
    shift_ref,
    img_hbm,
    txt_hbm,
    img_out_hbm,
    txt_out_hbm,
    img_ref,
    txt_ref,
    img_out,
    txt_out,
    imgs,
    txts,
    coefs,
    grads,
    text_sum,
    other_out,
    other_in,
    chain_out,
    chain_in,
    part_out,
    first_a,
    first_b,
    second,
    row_out,
    row_in,
    load_sem,
    store_sem,
    go_sem,
    relay_down,
    relay_up,
    send_sem,
    recv_sem,
):
    g = lax.axis_index("grp")
    q = lax.axis_index("loop")
    x = g // 4
    y = (g // 2) % 2
    core = g % 2
    z = q % ZS

    def member(xx, yy, cc):
        return {"grp": xx * 4 + yy * 2 + cc, "loop": q}

    twin = member(x, y, 1 - core)
    across = member(x, 1 - y, core)
    right = member((x + 1) % XS, y, core)
    left = member((x + XS - 1) % XS, y, core)
    below = {"grp": g, "loop": (q + loops - 1) % loops}
    above = {"grp": g, "loop": (q + 1) % loops}
    first_z = z == 0
    last_z = z == ZS - 1
    far_below = {"grp": across["grp"], "loop": below["loop"]}
    far_above = {"grp": across["grp"], "loop": above["loop"]}

    loads = [
        pltpu.make_async_copy(txt_hbm, txt_ref, load_sem.at[0]),
        pltpu.make_async_copy(img_hbm, img_ref, load_sem.at[1]),
    ]
    for load in loads:
        load.start()

    barrier = pltpu.get_barrier_semaphore()
    for peer in (twin, across, right, left):
        pl.semaphore_signal(barrier, inc=1, device_id=peer, device_id_type=MESH)

    @pl.when(first_z)
    def _():
        pl.semaphore_signal(barrier, inc=1, device_id=far_below, device_id_type=MESH)

    pl.semaphore_signal(barrier, inc=1, device_id=below, device_id_type=MESH)

    @pl.when(jnp.logical_not(last_z))
    def _():
        pl.semaphore_signal(barrier, inc=1, device_id=above, device_id_type=MESH)

    used = [0]

    def remote(src, dst, device, lands=None):
        i = used[0]
        used[0] += 1
        copy = pltpu.make_async_remote_copy(
            src_ref=src,
            dst_ref=dst,
            send_sem=send_sem.at[i],
            recv_sem=recv_sem.at[i if lands is None else lands],
            device_id=device,
            device_id_type=MESH,
        )
        return i, copy

    copies = []

    def link(src, dst, device):
        copies.append(remote(src, dst, device)[1])
        return copies[-1]

    class LoopLink:
        def __init__(self, src, dst, device, at_edge, relay, onto):
            self.at_edge, self.relay = at_edge, relay
            i, self.plain = remote(src, dst, device)
            if relay is not None:
                _, self.aside = remote(src, relay, across)
                _, self.onward = remote(relay, dst, onto, lands=i)
            copies.append(self)

        def start(self):
            if self.relay is None:
                self.plain.start()
            else:
                pl.when(jnp.logical_not(self.at_edge))(self.plain.start)
                pl.when(self.at_edge)(self.aside.start)

        def send_on(self):
            self.aside.wait_recv()
            self.onward.start()

        def wait_recv(self):
            self.plain.wait_recv()

        def wait_send(self):
            if self.relay is None:
                self.plain.wait_send()
                return
            pl.when(jnp.logical_not(self.at_edge))(self.plain.wait_send)

            @pl.when(self.at_edge)
            def _():
                self.aside.wait_send()
                self.onward.wait_send()

    down = {
        (h, c): LoopLink(
            imgs.at[h - 1, 0, half(c)],
            imgs.at[h, 0, half(c)],
            below,
            first_z,
            relay_down.at[h - 1, half(c)],
            far_below,
        )
        for h in range(1, HOPS + 1)
        for c in range(2)
    }
    to_twin = {
        (h, c): link(imgs.at[h, 0, half(c)], imgs.at[h, 1, half(c)], twin)
        for h in range(HOPS + 1)
        for c in range(2)
    }
    text_y = [link(txts.at[0, 0, half(c)], txts.at[1, 0, half(c)], across) for c in range(2)]
    text_right = {
        (r, c): link(txts.at[r, 0, half(c)], txts.at[r, 3, half(c)], right)
        for r in range(2)
        for c in range(2)
    }
    text_left = {
        (r, c): link(txts.at[r, 0, half(c)], txts.at[r, 1, half(c)], left)
        for r in range(2)
        for c in range(2)
    }
    text_far_a = [link(txts.at[r, 3, half(0)], txts.at[r, 2, half(0)], right) for r in range(2)]
    text_far_b = [link(txts.at[r, 1, half(1)], txts.at[r, 2, half(1)], left) for r in range(2)]
    term = {
        (h, c): link(other_out.at[h, half(c)], other_in.at[h, half(c)], twin)
        for h in range(HOPS + 1)
        for c in range(2)
    }
    up = {
        (h, u): LoopLink(
            chain_out.at[h - 1, sliver(u)],
            chain_in.at[h - 1, sliver(u)],
            above,
            last_z,
            relay_up.at[h - 1, sliver(u)] if u % 2 else None,
            far_above,
        )
        for h in range(1, HOPS + 1)
        for u in range(SLICES)
    }
    far_a = [link(part_out.at[r, 2, half(0)], first_a.at[r], right) for r in range(2)]
    far_b = [link(part_out.at[r, 2, half(1)], first_b.at[r], left) for r in range(2)]
    near_right = {
        (r, c): link(part_out.at[r, 1, half(c)], second.at[r, 0, half(c)], right)
        for r in range(2)
        for c in range(2)
    }
    near_left = {
        (r, c): link(part_out.at[r, 3, half(c)], second.at[r, 1, half(c)], left)
        for r in range(2)
        for c in range(2)
    }
    over = [link(row_out.at[half(c)], row_in.at[half(c)], across) for c in range(2)]
    assert used[0] == N_COPIES

    factor = factor_ref[0]
    shift = shift_ref[0]

    loads[0].wait()
    inv_txt = inverse_norm(txt_ref)
    txts[0, 0] = (txt_ref[...].astype(F32) * inv_txt).astype(BF16)
    loads[1].wait()
    inv_img = inverse_norm(img_ref)
    imgs[0, 0] = (img_ref[...].astype(F32) * inv_img).astype(BF16)

    @pl.when(first_z)
    def _():
        pl.semaphore_wait(barrier, 5)

    @pl.when(jnp.logical_not(jnp.logical_or(first_z, last_z)))
    def _():
        pl.semaphore_wait(barrier, 6)

    @pl.when(last_z)
    def _():
        pl.semaphore_wait(barrier, 7)
        pl.semaphore_signal(go_sem, inc=1, device_id=far_above, device_id_type=MESH)

    for c in range(2):
        text_y[c].start()
        pl.when(jnp.logical_not(first_z))(down[1, c].start)
        text_right[0, c].start()
        text_left[0, c].start()
    for c in range(2):
        to_twin[0, c].start()

    def pass_on(h, c):
        down[h, c].wait_recv()
        if h < HOPS:
            down[h + 1, c].start()
        to_twin[h, c].start()

    def send_on(links, at_edge, *keys):
        @pl.when(at_edge)
        def _():
            for key in keys:
                links[key].send_on()

    down_on = functools.partial(send_on, down, first_z)
    up_on = functools.partial(send_on, up, last_z)

    def from_twin(h):
        for c in range(2):
            to_twin[h, c].wait_recv()

    def spread_row(c):
        text_y[c].wait_recv()
        text_right[1, c].start()
        text_left[1, c].start()

    def coef_of(s):
        return jax.nn.sigmoid(s * factor + shift) * factor

    def scores(pictures):
        return lax.dot_general(
            pictures, txts[...].reshape(WORDS, WIDE), BOTH_LAST, preferred_element_type=F32
        )

    def coef_hops(lo, hi):
        s = scores(imgs[lo:hi].reshape((hi - lo) * 2 * ROWS, WIDE))
        coefs[lo:hi] = coef_of(s).astype(BF16).reshape(hi - lo, 2, ROWS, WORDS)
        if lo == 0:
            own = s[0:ROWS, 0:128] * factor + shift
            rows = lax.broadcasted_iota(jnp.int32, own.shape, 0)
            cols = lax.broadcasted_iota(jnp.int32, own.shape, 1)
            sign = jnp.where(rows == cols, 1.0, -1.0).astype(F32)
            value = -sign * jax.nn.sigmoid(-sign * own) * factor
            coefs[0, 0, :, 0:128] = value.astype(BF16)

    def coef_half(h, c):
        s = scores(imgs[h, :, c * HALF : (c + 1) * HALF].reshape(2 * HALF, WIDE))
        coefs[h, :, c * HALF : (c + 1) * HALF] = coef_of(s).astype(BF16).reshape(2, HALF, WORDS)

    def terms_hops(lo, hi):
        out = jnp.dot(
            coefs[lo:hi].reshape((hi - lo) * 2 * ROWS, WORDS),
            txts[...].reshape(WORDS, WIDE),
            preferred_element_type=F32,
        ).reshape(hi - lo, 2, ROWS, WIDE)
        grads[lo:hi] = out[:, 0]
        other_out[lo:hi] = out[:, 1].astype(BF16)
        for h in range(lo, hi):
            for c in range(2):
                term[h, c].start()

    def terms_half(h, c):
        out = jnp.dot(
            coefs[h, :, c * HALF : (c + 1) * HALF].reshape(2 * HALF, WORDS),
            txts[...].reshape(WORDS, WIDE),
            preferred_element_type=F32,
        ).reshape(2, HALF, WIDE)
        grads[h, half(c)] = out[0]
        other_out[h, half(c)] = out[1].astype(BF16)
        term[h, c].start()

    def climb(h, u):
        if u % 2 == 0:
            term[h, u // 2].wait_recv()
        total = grads[h, sliver(u)] + other_in[h, sliver(u)].astype(F32)
        if h < HOPS:
            up[h + 1, u].wait_recv()
            total = total + chain_in[h, sliver(u)].astype(F32)
        if h > 0:
            chain_out[h - 1, sliver(u)] = total.astype(BF16)
            up[h, u].start()
        else:
            grads[0, sliver(u)] = total

    spread_row(0)

    pl.when(first_z)(down[1, 0].start)
    pass_on(1, 0)
    spread_row(1)
    pl.when(first_z)(down[1, 1].start)
    text_right[0, 0].wait_recv()
    text_far_a[0].start()
    text_left[0, 1].wait_recv()
    text_far_b[0].start()
    pass_on(1, 1)

    @pl.when(first_z)
    def _():
        pl.semaphore_wait(go_sem, 1)

    down_on((1, 0), (1, 1))

    def far_text(side):
        (text_right[1, 0] if side == 0 else text_left[1, 1]).wait_recv()
        (text_far_a[1] if side == 0 else text_far_b[1]).start()

    pl.when(last_z)(functools.partial(far_text, 0))
    pass_on(2, 0)
    pl.when(jnp.logical_not(last_z))(functools.partial(far_text, 0))
    pl.when(last_z)(functools.partial(far_text, 1))
    pass_on(2, 1)
    pl.when(jnp.logical_not(last_z))(functools.partial(far_text, 1))

    down_on((2, 0), (2, 1))
    pass_on(3, 0)
    down_on((3, 0))
    pass_on(3, 1)
    down_on((3, 1))
    text_right[0, 1].wait_recv()
    text_left[0, 0].wait_recv()
    text_right[1, 1].wait_recv()
    text_left[1, 0].wait_recv()
    for r in range(2):
        text_far_a[r].wait_recv()
        text_far_b[r].wait_recv()
    for h in range(2):
        from_twin(h)
    coef_hops(0, 2)
    pass_on(4, 0)
    down_on((4, 0))
    for h in range(2, 4):
        from_twin(h)
    coef_hops(2, 4)
    down_on((4, 1))
    to_twin[4, 0].wait_recv()
    coef_half(4, 0)
    terms_half(4, 0)
    pass_on(4, 1)
    terms_hops(0, 4)
    climb(4, 0)
    climb(4, 1)

    def text_row(r, lo, hi):
        at = r * MINE
        total = lax.dot_general(
            coefs[lo:hi, :, :, at : at + MINE].reshape((hi - lo) * 2 * ROWS, MINE),
            imgs[lo:hi].reshape((hi - lo) * 2 * ROWS, WIDE),
            BOTH_FIRST,
            preferred_element_type=F32,
        )
        if lo > 0:
            total = text_sum[at : at + MINE] + total
        text_sum[at : at + MINE] = total
        if hi > HOPS:
            part_out[r] = total.astype(BF16).reshape(XS, ROWS, WIDE)

    def join(r):
        far_a[r].wait_recv()
        at = (r * XS + 1) * ROWS
        part_out[r, 1, half(0)] = (text_sum[at : at + HALF] + first_a[r].astype(F32)).astype(BF16)
        near_right[r, 0].start()
        far_b[r].wait_recv()
        at = (r * XS + 3) * ROWS + HALF
        part_out[r, 3, half(1)] = (text_sum[at : at + HALF] + first_b[r].astype(F32)).astype(BF16)
        near_left[r, 1].start()

    def row_total(r, c):
        near_right[r, c].wait_recv()
        near_left[r, c].wait_recv()
        at = r * MINE + c * HALF
        return (
            text_sum[at : at + HALF]
            + second[r, 0, half(c)].astype(F32)
            + second[r, 1, half(c)].astype(F32)
        )

    def join_rows():
        join(1)
        near_right[0, 1].start()
        near_left[0, 0].start()

    def store(ref, hbm, rows, i):
        copy = pltpu.make_async_copy(ref.at[rows], hbm.at[rows], store_sem.at[i])
        copy.start()
        return copy

    def image_result(c):
        rows = slice(c * HALF, (c + 1) * HALF)
        img_out[rows] = back_norm(img_ref[rows], inv_img[rows], grads[0, rows])
        return store(img_out, img_out_hbm, half(c), c)

    text_row(1, 0, HOPS)
    to_twin[4, 1].wait_recv()
    coef_half(4, 1)
    text_row(1, HOPS, HOPS + 1)
    far_a[1].start()
    far_b[1].start()
    near_right[1, 1].start()
    near_left[1, 0].start()
    terms_half(4, 1)
    text_row(0, 0, HOPS + 1)
    far_a[0].start()
    far_b[0].start()
    up_on((4, 1))
    climb(4, 2)
    climb(4, 3)

    def sum_row():
        for c in range(2):
            row_out[half(c)] = row_total(1, c).astype(BF16)
            over[c].start()

    def own_row():
        for c in range(2):
            text_sum[c * HALF : (c + 1) * HALF] = row_total(0, c)

    steps = (join_rows, functools.partial(join, 0), sum_row, own_row)

    usual = (1, 2, 3, 4)
    moved = ({0: 0}, {0: 0, 1: 1}, {0: 1, 1: 2, 2: 2, ZS - 1: 4}, {0: 2, 1: 3, 2: 3, 3: 3})

    def at_place(place):
        for step, common, others in zip(steps, usual, moved):
            if place == common:
                here = functools.reduce(jnp.logical_and, [z != at for at in others if others[at] != place])
                pl.when(here)(step)
            else:
                chosen = [z == at for at in others if others[at] == place]
                if chosen:
                    pl.when(functools.reduce(jnp.logical_or, chosen))(step)

    at_place(0)
    climb(3, 0)
    climb(3, 1)
    at_place(1)
    up_on((4, 3), (3, 1))
    climb(2, 0)
    climb(2, 1)
    climb(3, 2)
    climb(3, 3)
    at_place(2)
    up_on((2, 1), (3, 3))
    climb(1, 0)
    climb(1, 1)
    climb(2, 2)
    climb(2, 3)
    at_place(3)
    up_on((1, 1))
    climb(0, 0)
    climb(0, 1)
    stores = [image_result(0)]
    up_on((2, 3))
    climb(1, 2)
    climb(1, 3)
    up_on((1, 3))
    at_place(4)
    for c in range(2):
        over[c].wait_recv()
    txt_out[...] = back_norm(txt_ref[...], inv_txt, text_sum[0:ROWS] + row_in[...].astype(F32))
    stores.append(store(txt_out, txt_out_hbm, pl.ds(0, ROWS), 2))
    climb(0, 2)
    climb(0, 3)
    stores.append(image_result(1))

    for copy in copies:
        copy.wait_send()
    for copy in stores:
        copy.wait()


N_COPIES = 3 * 8 + 10 + 2 + 4 + 4 + 2 + 2 + 10 + 2 * 16 + 2 + 2 + 4 + 4 + 2


def per_device(loops, images, texts, factor, shift):
    smem = pl.BlockSpec(memory_space=pltpu.SMEM)
    hbm = pl.BlockSpec(memory_space=pl.ANY)
    out = jax.ShapeDtypeStruct((ROWS, WIDE), F32)
    return pl.pallas_call(
        functools.partial(kernel, loops),
        out_shape=(out, out),
        in_specs=[smem, smem, hbm, hbm],
        out_specs=(hbm, hbm),
        scratch_shapes=[
            pltpu.VMEM((ROWS, WIDE), BF16),
            pltpu.VMEM((ROWS, WIDE), BF16),
            pltpu.VMEM((ROWS, WIDE), F32),
            pltpu.VMEM((ROWS, WIDE), F32),
            pltpu.VMEM((HOPS + 1, 2, ROWS, WIDE), BF16),
            pltpu.VMEM((2, XS, ROWS, WIDE), BF16),
            pltpu.VMEM((HOPS + 1, 2, ROWS, WORDS), BF16),
            pltpu.VMEM((HOPS + 1, ROWS, WIDE), F32),
            pltpu.VMEM((WORDS, WIDE), F32),
            pltpu.VMEM((HOPS + 1, ROWS, WIDE), BF16),
            pltpu.VMEM((HOPS + 1, ROWS, WIDE), BF16),
            pltpu.VMEM((HOPS, ROWS, WIDE), BF16),
            pltpu.VMEM((HOPS, ROWS, WIDE), BF16),
            pltpu.VMEM((2, XS, ROWS, WIDE), BF16),
            pltpu.VMEM((2, HALF, WIDE), BF16),
            pltpu.VMEM((2, HALF, WIDE), BF16),
            pltpu.VMEM((2, 2, ROWS, WIDE), BF16),
            pltpu.VMEM((ROWS, WIDE), BF16),
            pltpu.VMEM((ROWS, WIDE), BF16),
            pltpu.SemaphoreType.DMA((2,)),
            pltpu.SemaphoreType.DMA((3,)),
            pltpu.SemaphoreType.REGULAR,
            pltpu.VMEM((HOPS, ROWS, WIDE), BF16),
            pltpu.VMEM((HOPS, ROWS, WIDE), BF16),
            pltpu.SemaphoreType.DMA((N_COPIES,)),
            pltpu.SemaphoreType.DMA((N_COPIES,)),
        ],
        compiler_params=pltpu.CompilerParams(
            collective_id=0, has_side_effects=True, vmem_limit_bytes=60 * 2**20
        ),
        name="siglip",
    )(factor, shift, images, texts)


def solution(mesh):
    loops = mesh.shape["loop"]
    spec = P(("grp", "loop"), None)

    def step(images, texts, factor, shift):
        return per_device(loops, images, texts, factor, shift)

    return jax.shard_map(
        step, mesh=mesh, in_specs=(spec, spec, P(), P()), out_specs=(spec, spec), check_vma=False
    )
```

```python
import functools

import jax
import jax.numpy as jnp
from jax import lax
from jax.experimental import pallas as pl
from jax.experimental.pallas import tpu as pltpu
from jax.sharding import PartitionSpec as P

HOPS = 4
ROWS = 64
HALF = 32
SLICE = 16
SLICES = ROWS // SLICE
WIDE = 1536
XS = 4
ZS = 16
MINE = XS * ROWS
WORDS = 2 * MINE
MESH = pl.DeviceIdType.MESH
F32 = jnp.float32
BF16 = jnp.bfloat16
BOTH_LAST = (((1,), (1,)), ((), ()))
BOTH_FIRST = (((0,), (0,)), ((), ()))


def half(c):
    return pl.ds(c * HALF, HALF)


def sliver(u):
    return pl.ds(u * SLICE, SLICE)


def inverse_norm(ref):
    wide = ref[...].astype(F32)
    return lax.rsqrt(jnp.sum(wide * wide, axis=-1, keepdims=True) + 1e-06)


def back_norm(raw, inverse, grad):
    unit = raw.astype(F32) * inverse
    return (grad - unit * jnp.sum(unit * grad, axis=-1, keepdims=True)) * inverse


def kernel(
    loops,
    factor_ref,
    shift_ref,
    img_hbm,
    txt_hbm,
    img_out,
    txt_out,
    img_ref,
    txt_ref,
    imgs,
    txts,
    coefs,
    grads,
    text_sum,
    other_out,
    other_in,
    chain_out,
    chain_in,
    part_out,
    first_a,
    first_b,
    second,
    row_out,
    row_in,
    load_sem,
    go_sem,
    relay_down,
    relay_up,
    send_sem,
    recv_sem,
):
    g = lax.axis_index("grp")
    q = lax.axis_index("loop")
    x = g // 4
    y = (g // 2) % 2
    core = g % 2
    z = q % ZS

    def member(xx, yy, cc):
        return {"grp": xx * 4 + yy * 2 + cc, "loop": q}

    twin = member(x, y, 1 - core)
    across = member(x, 1 - y, core)
    right = member((x + 1) % XS, y, core)
    left = member((x + XS - 1) % XS, y, core)
    below = {"grp": g, "loop": (q + loops - 1) % loops}
    above = {"grp": g, "loop": (q + 1) % loops}
    first_z = z == 0
    last_z = z == ZS - 1
    far_below = {"grp": across["grp"], "loop": below["loop"]}
    far_above = {"grp": across["grp"], "loop": above["loop"]}

    loads = [
        pltpu.make_async_copy(txt_hbm, txt_ref, load_sem.at[0]),
        pltpu.make_async_copy(img_hbm, img_ref, load_sem.at[1]),
    ]
    for load in loads:
        load.start()

    barrier = pltpu.get_barrier_semaphore()
    for peer in (twin, across, right, left):
        pl.semaphore_signal(barrier, inc=1, device_id=peer, device_id_type=MESH)

    @pl.when(first_z)
    def _():
        pl.semaphore_signal(barrier, inc=1, device_id=far_below, device_id_type=MESH)

    pl.semaphore_signal(barrier, inc=1, device_id=below, device_id_type=MESH)

    @pl.when(jnp.logical_not(last_z))
    def _():
        pl.semaphore_signal(barrier, inc=1, device_id=above, device_id_type=MESH)

    used = [0]

    def remote(src, dst, device, lands=None):
        i = used[0]
        used[0] += 1
        copy = pltpu.make_async_remote_copy(
            src_ref=src,
            dst_ref=dst,
            send_sem=send_sem.at[i],
            recv_sem=recv_sem.at[i if lands is None else lands],
            device_id=device,
            device_id_type=MESH,
        )
        return i, copy

    copies = []

    def link(src, dst, device):
        copies.append(remote(src, dst, device)[1])
        return copies[-1]

    class LoopLink:
        def __init__(self, src, dst, device, at_edge, relay, onto):
            self.at_edge, self.relay = at_edge, relay
            i, self.plain = remote(src, dst, device)
            if relay is not None:
                _, self.aside = remote(src, relay, across)
                _, self.onward = remote(relay, dst, onto, lands=i)
            copies.append(self)

        def start(self):
            if self.relay is None:
                self.plain.start()
            else:
                pl.when(jnp.logical_not(self.at_edge))(self.plain.start)
                pl.when(self.at_edge)(self.aside.start)

        def send_on(self):
            self.aside.wait_recv()
            self.onward.start()

        def wait_recv(self):
            self.plain.wait_recv()

        def wait_send(self):
            if self.relay is None:
                self.plain.wait_send()
                return
            pl.when(jnp.logical_not(self.at_edge))(self.plain.wait_send)

            @pl.when(self.at_edge)
            def _():
                self.aside.wait_send()
                self.onward.wait_send()

    down = {
        (h, c): LoopLink(
            imgs.at[h - 1, 0, half(c)],
            imgs.at[h, 0, half(c)],
            below,
            first_z,
            relay_down.at[h - 1, half(c)],
            far_below,
        )
        for h in range(1, HOPS + 1)
        for c in range(2)
    }
    to_twin = {
        (h, c): link(imgs.at[h, 0, half(c)], imgs.at[h, 1, half(c)], twin)
        for h in range(HOPS + 1)
        for c in range(2)
    }
    text_y = [link(txts.at[0, 0, half(c)], txts.at[1, 0, half(c)], across) for c in range(2)]
    text_right = {
        (r, c): link(txts.at[r, 0, half(c)], txts.at[r, 3, half(c)], right)
        for r in range(2)
        for c in range(2)
    }
    text_left = {
        (r, c): link(txts.at[r, 0, half(c)], txts.at[r, 1, half(c)], left)
        for r in range(2)
        for c in range(2)
    }
    text_far_a = [link(txts.at[r, 3, half(0)], txts.at[r, 2, half(0)], right) for r in range(2)]
    text_far_b = [link(txts.at[r, 1, half(1)], txts.at[r, 2, half(1)], left) for r in range(2)]
    term = {
        (h, c): link(other_out.at[h, half(c)], other_in.at[h, half(c)], twin)
        for h in range(HOPS + 1)
        for c in range(2)
    }
    up = {
        (h, u): LoopLink(
            chain_out.at[h - 1, sliver(u)],
            chain_in.at[h - 1, sliver(u)],
            above,
            last_z,
            relay_up.at[h - 1, sliver(u)] if u % 2 else None,
            far_above,
        )
        for h in range(1, HOPS + 1)
        for u in range(SLICES)
    }
    far_a = [link(part_out.at[r, 2, half(0)], first_a.at[r], right) for r in range(2)]
    far_b = [link(part_out.at[r, 2, half(1)], first_b.at[r], left) for r in range(2)]
    near_right = {
        (r, c): link(part_out.at[r, 1, half(c)], second.at[r, 0, half(c)], right)
        for r in range(2)
        for c in range(2)
    }
    near_left = {
        (r, c): link(part_out.at[r, 3, half(c)], second.at[r, 1, half(c)], left)
        for r in range(2)
        for c in range(2)
    }
    over = [link(row_out.at[half(c)], row_in.at[half(c)], across) for c in range(2)]
    assert used[0] == N_COPIES

    factor = factor_ref[0]
    shift = shift_ref[0]

    @pl.when(last_z)
    def _():
        pl.semaphore_wait(barrier, 7)
        pl.semaphore_signal(go_sem, inc=1, device_id=far_above, device_id_type=MESH)

    loads[0].wait()
    inv_txt = inverse_norm(txt_ref)
    txts[0, 0] = (txt_ref[...].astype(F32) * inv_txt).astype(BF16)
    loads[1].wait()
    inv_img = inverse_norm(img_ref)
    imgs[0, 0] = (img_ref[...].astype(F32) * inv_img).astype(BF16)

    @pl.when(first_z)
    def _():
        pl.semaphore_wait(barrier, 5)

    @pl.when(jnp.logical_not(jnp.logical_or(first_z, last_z)))
    def _():
        pl.semaphore_wait(barrier, 6)

    for c in range(2):
        text_y[c].start()
        pl.when(jnp.logical_not(first_z))(down[1, c].start)
        text_right[0, c].start()
        text_left[0, c].start()
    for c in range(2):
        pl.when(first_z)(down[1, c].start)
    for c in range(2):
        to_twin[0, c].start()

    def pass_on(h, c):
        down[h, c].wait_recv()
        if h == 1:
            pl.when(jnp.logical_not(first_z))(down[2, c].start)
        elif h < HOPS:
            down[h + 1, c].start()
        to_twin[h, c].start()

    def send_on(links, at_edge, *keys):
        @pl.when(at_edge)
        def _():
            for key in keys:
                links[key].send_on()

    down_on = functools.partial(send_on, down, first_z)
    up_on = functools.partial(send_on, up, last_z)

    def from_twin(h):
        for c in range(2):
            to_twin[h, c].wait_recv()

    def spread_row(c):
        text_y[c].wait_recv()
        text_right[1, c].start()
        text_left[1, c].start()

    def coef_of(s):
        return jax.nn.sigmoid(s * factor + shift) * factor

    def scores(pictures):
        return lax.dot_general(
            pictures, txts[...].reshape(WORDS, WIDE), BOTH_LAST, preferred_element_type=F32
        )

    def coef_hops(lo, hi):
        s = scores(imgs[lo:hi].reshape((hi - lo) * 2 * ROWS, WIDE))
        coefs[lo:hi] = coef_of(s).astype(BF16).reshape(hi - lo, 2, ROWS, WORDS)
        if lo == 0:
            own = s[0:ROWS, 0:128] * factor + shift
            rows = lax.broadcasted_iota(jnp.int32, own.shape, 0)
            cols = lax.broadcasted_iota(jnp.int32, own.shape, 1)
            sign = jnp.where(rows == cols, 1.0, -1.0).astype(F32)
            value = -sign * jax.nn.sigmoid(-sign * own) * factor
            coefs[0, 0, :, 0:128] = value.astype(BF16)

    def coef_half(h, c):
        s = scores(imgs[h, :, c * HALF : (c + 1) * HALF].reshape(2 * HALF, WIDE))
        coefs[h, :, c * HALF : (c + 1) * HALF] = coef_of(s).astype(BF16).reshape(2, HALF, WORDS)

    def terms_hops(lo, hi):
        out = jnp.dot(
            coefs[lo:hi].reshape((hi - lo) * 2 * ROWS, WORDS),
            txts[...].reshape(WORDS, WIDE),
            preferred_element_type=F32,
        ).reshape(hi - lo, 2, ROWS, WIDE)
        grads[lo:hi] = out[:, 0]
        other_out[lo:hi] = out[:, 1].astype(BF16)
        for h in range(lo, hi):
            for c in range(2):
                term[h, c].start()

    def terms_half(h, c):
        out = jnp.dot(
            coefs[h, :, c * HALF : (c + 1) * HALF].reshape(2 * HALF, WORDS),
            txts[...].reshape(WORDS, WIDE),
            preferred_element_type=F32,
        ).reshape(2, HALF, WIDE)
        grads[h, half(c)] = out[0]
        other_out[h, half(c)] = out[1].astype(BF16)
        term[h, c].start()

    def climb(h, u):
        if u % 2 == 0:
            term[h, u // 2].wait_recv()
        total = grads[h, sliver(u)] + other_in[h, sliver(u)].astype(F32)
        if h < HOPS:
            up[h + 1, u].wait_recv()
            total = total + chain_in[h, sliver(u)].astype(F32)
        if h > 0:
            chain_out[h - 1, sliver(u)] = total.astype(BF16)
            up[h, u].start()
        else:
            grads[0, sliver(u)] = total

    spread_row(0)

    pass_on(1, 0)
    spread_row(1)
    text_right[0, 0].wait_recv()
    text_far_a[0].start()
    text_left[0, 1].wait_recv()
    text_far_b[0].start()
    pass_on(1, 1)

    @pl.when(first_z)
    def _():
        down[2, 0].start()
        pl.semaphore_wait(go_sem, 1)

    down_on((1, 0), (1, 1))
    pl.when(first_z)(down[2, 1].start)

    def far_text(side):
        (text_right[1, 0] if side == 0 else text_left[1, 1]).wait_recv()
        (text_far_a[1] if side == 0 else text_far_b[1]).start()

    pl.when(last_z)(functools.partial(far_text, 0))
    pass_on(2, 0)
    pl.when(jnp.logical_not(last_z))(functools.partial(far_text, 0))
    pl.when(last_z)(functools.partial(far_text, 1))
    pass_on(2, 1)
    pl.when(jnp.logical_not(last_z))(functools.partial(far_text, 1))

    down_on((2, 0), (2, 1))
    pass_on(3, 0)
    down_on((3, 0))
    pass_on(3, 1)
    down_on((3, 1))
    text_right[0, 1].wait_recv()
    text_left[0, 0].wait_recv()
    text_right[1, 1].wait_recv()
    text_left[1, 0].wait_recv()
    for r in range(2):
        text_far_a[r].wait_recv()
        text_far_b[r].wait_recv()
    for h in range(2):
        from_twin(h)
    coef_hops(0, 2)
    pass_on(4, 0)
    down_on((4, 0))
    for h in range(2, 4):
        from_twin(h)
    coef_hops(2, 4)
    down_on((4, 1))
    to_twin[4, 0].wait_recv()
    coef_half(4, 0)
    terms_half(4, 0)
    pass_on(4, 1)
    terms_hops(0, 4)
    climb(4, 0)
    climb(4, 1)

    def text_row(r):
        at = r * MINE
        total = lax.dot_general(
            coefs[:, :, :, at : at + MINE].reshape((HOPS + 1) * 2 * ROWS, MINE),
            imgs[...].reshape((HOPS + 1) * 2 * ROWS, WIDE),
            BOTH_FIRST,
            preferred_element_type=F32,
        )
        text_sum[at : at + MINE] = total
        part_out[r] = total.astype(BF16).reshape(XS, ROWS, WIDE)

    def join(r):
        far_a[r].wait_recv()
        at = (r * XS + 1) * ROWS
        part_out[r, 1, half(0)] = (text_sum[at : at + HALF] + first_a[r].astype(F32)).astype(BF16)
        near_right[r, 0].start()
        far_b[r].wait_recv()
        at = (r * XS + 3) * ROWS + HALF
        part_out[r, 3, half(1)] = (text_sum[at : at + HALF] + first_b[r].astype(F32)).astype(BF16)
        near_left[r, 1].start()

    def row_total(r, c):
        near_right[r, c].wait_recv()
        near_left[r, c].wait_recv()
        at = r * MINE + c * HALF
        return (
            text_sum[at : at + HALF]
            + second[r, 0, half(c)].astype(F32)
            + second[r, 1, half(c)].astype(F32)
        )

    def join_rows():
        join(1)
        near_right[0, 1].start()
        near_left[0, 0].start()

    def image_result(c):
        rows = slice(c * HALF, (c + 1) * HALF)
        img_out[rows] = back_norm(img_ref[rows], inv_img[rows], grads[0, rows])

    to_twin[4, 1].wait_recv()
    coef_half(4, 1)
    terms_half(4, 1)
    text_row(1)
    far_a[1].start()
    far_b[1].start()
    near_right[1, 1].start()
    near_left[1, 0].start()
    up_on((4, 1))
    climb(4, 2)
    climb(4, 3)
    text_row(0)
    far_a[0].start()
    far_b[0].start()

    def sum_row():
        for c in range(2):
            row_out[half(c)] = row_total(1, c).astype(BF16)
            over[c].start()

    def own_row():
        for c in range(2):
            text_sum[c * HALF : (c + 1) * HALF] = row_total(0, c)

    steps = (join_rows, functools.partial(join, 0), sum_row, own_row)

    usual = (1, 2, 3, 4)
    moved = ({0: 0}, {0: 0, 1: 1}, {0: 1, 1: 2, 2: 2, ZS - 1: 4}, {0: 2, 1: 3, 2: 3, 3: 3})

    def at_place(place):
        for step, common, others in zip(steps, usual, moved):
            if place == common:
                here = functools.reduce(jnp.logical_and, [z != at for at in others if others[at] != place])
                pl.when(here)(step)
            else:
                chosen = [z == at for at in others if others[at] == place]
                if chosen:
                    pl.when(functools.reduce(jnp.logical_or, chosen))(step)

    at_place(0)
    climb(3, 0)
    climb(3, 1)
    at_place(1)
    climb(3, 2)
    climb(3, 3)
    up_on((4, 3), (3, 1))
    climb(2, 0)
    climb(2, 1)
    at_place(2)
    up_on((3, 3))
    climb(2, 2)
    climb(2, 3)
    up_on((2, 1))
    climb(1, 0)
    climb(1, 1)
    at_place(3)
    climb(1, 2)
    climb(1, 3)
    up_on((2, 3), (1, 1))
    climb(0, 0)
    climb(0, 1)
    image_result(0)
    up_on((1, 3))
    at_place(4)
    for c in range(2):
        over[c].wait_recv()
    txt_out[...] = back_norm(txt_ref[...], inv_txt, text_sum[0:ROWS] + row_in[...].astype(F32))
    climb(0, 2)
    climb(0, 3)
    image_result(1)

    for copy in copies:
        copy.wait_send()


N_COPIES = 3 * 8 + 10 + 2 + 4 + 4 + 2 + 2 + 10 + 2 * 16 + 2 + 2 + 4 + 4 + 2


def per_device(loops, images, texts, factor, shift):
    smem = pl.BlockSpec(memory_space=pltpu.SMEM)
    hbm = pl.BlockSpec(memory_space=pltpu.HBM)
    vmem = pl.BlockSpec(memory_space=pltpu.VMEM)
    out = jax.ShapeDtypeStruct((ROWS, WIDE), F32)
    return pl.pallas_call(
        functools.partial(kernel, loops),
        out_shape=(out, out),
        in_specs=[smem, smem, hbm, hbm],
        out_specs=(vmem, vmem),
        scratch_shapes=[
            pltpu.VMEM((ROWS, WIDE), BF16),
            pltpu.VMEM((ROWS, WIDE), BF16),
            pltpu.VMEM((HOPS + 1, 2, ROWS, WIDE), BF16),
            pltpu.VMEM((2, XS, ROWS, WIDE), BF16),
            pltpu.VMEM((HOPS + 1, 2, ROWS, WORDS), BF16),
            pltpu.VMEM((HOPS + 1, ROWS, WIDE), F32),
            pltpu.VMEM((WORDS, WIDE), F32),
            pltpu.VMEM((HOPS + 1, ROWS, WIDE), BF16),
            pltpu.VMEM((HOPS + 1, ROWS, WIDE), BF16),
            pltpu.VMEM((HOPS, ROWS, WIDE), BF16),
            pltpu.VMEM((HOPS, ROWS, WIDE), BF16),
            pltpu.VMEM((2, XS, ROWS, WIDE), BF16),
            pltpu.VMEM((2, HALF, WIDE), BF16),
            pltpu.VMEM((2, HALF, WIDE), BF16),
            pltpu.VMEM((2, 2, ROWS, WIDE), BF16),
            pltpu.VMEM((ROWS, WIDE), BF16),
            pltpu.VMEM((ROWS, WIDE), BF16),
            pltpu.SemaphoreType.DMA((2,)),
            pltpu.SemaphoreType.REGULAR,
            pltpu.VMEM((HOPS, ROWS, WIDE), BF16),
            pltpu.VMEM((HOPS, ROWS, WIDE), BF16),
            pltpu.SemaphoreType.DMA((N_COPIES,)),
            pltpu.SemaphoreType.DMA((N_COPIES,)),
        ],
        compiler_params=pltpu.CompilerParams(
            collective_id=0, has_side_effects=True, vmem_limit_bytes=48 * 2**20
        ),
        name="siglip",
    )(
        factor,
        shift,
        pltpu.with_memory_space_constraint(images, pltpu.HBM),
        pltpu.with_memory_space_constraint(texts, pltpu.HBM),
    )


def solution(mesh):
    loops = mesh.shape["loop"]
    spec = P(("grp", "loop"), None)

    def step(images, texts, factor, shift):
        return per_device(loops, images, texts, factor, shift)

    return jax.shard_map(
        step, mesh=mesh, in_specs=(spec, spec, P(), P()), out_specs=(spec, spec), check_vma=False
    )
```

```python
import functools

import jax
import jax.numpy as jnp
from jax import lax
from jax.experimental import pallas as pl
from jax.experimental.pallas import tpu as pltpu
from jax.sharding import PartitionSpec as P

HOPS = 4
ROWS = 64
HALF = 32
SLICE = 16
SLICES = ROWS // SLICE
WIDE = 1536
XS = 4
ZS = 16
MINE = XS * ROWS
WORDS = 2 * MINE
DOWN, UP, TWIN, TEXT, PART = 0, 2, 4, 5, 6
N_LEAVES = 7
MESH = pl.DeviceIdType.MESH
F32 = jnp.float32
BF16 = jnp.bfloat16
BOTH_LAST = (((1,), (1,)), ((), ()))
BOTH_FIRST = (((0,), (0,)), ((), ()))


def half(c):
    return pl.ds(c * HALF, HALF)


def sliver(u):
    return pl.ds(u * SLICE, SLICE)


def inverse_norm(ref):
    wide = ref[...].astype(F32)
    return lax.rsqrt(jnp.sum(wide * wide, axis=-1, keepdims=True) + 1e-06)


def back_norm(raw, inverse, grad):
    unit = raw.astype(F32) * inverse
    return (grad - unit * jnp.sum(unit * grad, axis=-1, keepdims=True)) * inverse


def kernel(
    loops,
    factor_ref,
    shift_ref,
    img_hbm,
    txt_hbm,
    img_out,
    txt_out,
    img_ref,
    txt_ref,
    imgs,
    txts,
    coefs,
    grads,
    text_sum,
    other_out,
    other_in,
    chain_out,
    chain_in,
    part_out,
    first_a,
    first_b,
    second,
    row_out,
    row_in,
    load_sem,
    go_sem,
    relay_down,
    relay_up,
    send_sem,
    recv_sem,
):
    g = lax.axis_index("grp")
    q = lax.axis_index("loop")
    x = g // 4
    y = (g // 2) % 2
    core = g % 2
    z = q % ZS

    def member(xx, yy, cc):
        return {"grp": xx * 4 + yy * 2 + cc, "loop": q}

    twin = member(x, y, 1 - core)
    across = member(x, 1 - y, core)
    right = member((x + 1) % XS, y, core)
    left = member((x + XS - 1) % XS, y, core)
    below = {"grp": g, "loop": (q + loops - 1) % loops}
    above = {"grp": g, "loop": (q + 1) % loops}
    first_z = z == 0
    last_z = z == ZS - 1
    far_below = {"grp": across["grp"], "loop": below["loop"]}
    far_above = {"grp": across["grp"], "loop": above["loop"]}

    loads = [
        pltpu.make_async_copy(txt_hbm, txt_ref, load_sem.at[0]),
        pltpu.make_async_copy(img_hbm, img_ref, load_sem.at[1]),
    ]
    for load in loads:
        load.start()

    barrier = pltpu.get_barrier_semaphore()
    for peer in (twin, across, right, left):
        pl.semaphore_signal(barrier, inc=1, device_id=peer, device_id_type=MESH)

    @pl.when(first_z)
    def _():
        pl.semaphore_signal(barrier, inc=1, device_id=far_below, device_id_type=MESH)

    pl.semaphore_signal(barrier, inc=1, device_id=below, device_id_type=MESH)

    @pl.when(jnp.logical_not(last_z))
    def _():
        pl.semaphore_signal(barrier, inc=1, device_id=above, device_id_type=MESH)

    used = [0]

    def arrival():
        used[0] += 1
        return used[0] - 1

    def remote(src, dst, device, leaves, lands):
        return pltpu.make_async_remote_copy(
            src_ref=src,
            dst_ref=dst,
            send_sem=send_sem.at[leaves],
            recv_sem=recv_sem.at[lands],
            device_id=device,
            device_id_type=MESH,
        )

    def link(src, dst, device, leaves, lands=None):
        return remote(src, dst, device, leaves, arrival() if lands is None else lands)

    class LoopLink:
        def __init__(self, src, dst, device, leaves, at_edge, relay, onto):
            self.at_edge, self.relay = at_edge, relay
            lands = arrival()
            self.plain = remote(src, dst, device, leaves, lands)
            if relay is not None:
                self.aside = remote(src, relay, across, leaves, arrival())
                self.onward = remote(relay, dst, onto, leaves + 1, lands)

        def start(self):
            if self.relay is None:
                self.plain.start()
            else:
                pl.when(jnp.logical_not(self.at_edge))(self.plain.start)
                pl.when(self.at_edge)(self.aside.start)

        def send_on(self):
            self.aside.wait_recv()
            self.onward.start()

        def wait_recv(self):
            self.plain.wait_recv()

    down = {
        (h, c): LoopLink(
            imgs.at[h - 1, 0, half(c)],
            imgs.at[h, 0, half(c)],
            below,
            DOWN,
            first_z,
            relay_down.at[h - 1, half(c)],
            far_below,
        )
        for h in range(1, HOPS + 1)
        for c in range(2)
    }
    to_twin = [link(imgs.at[0, 0], imgs.at[0, 1], twin, TWIN)]
    to_twin_half = {}
    for h in range(1, HOPS + 1):
        lands = arrival()
        for c in range(2):
            alone = lands if h < HOPS or c == 0 else arrival()
            to_twin_half[h, c] = link(
                imgs.at[h, 0, half(c)], imgs.at[h, 1, half(c)], twin, TWIN, alone
            )
        if h < HOPS:
            to_twin.append(link(imgs.at[h, 0], imgs.at[h, 1], twin, TWIN, lands))
    text_y = [
        link(txts.at[0, 0, half(c)], txts.at[1, 0, half(c)], across, TEXT) for c in range(2)
    ]
    text_last = arrival()
    text_right = {
        (r, c): link(
            txts.at[r, 0, half(c)],
            txts.at[r, 3, half(c)],
            right,
            TEXT,
            arrival() if c == 0 else text_last,
        )
        for r in range(2)
        for c in range(2)
    }
    text_left = {
        (r, c): link(
            txts.at[r, 0, half(c)],
            txts.at[r, 1, half(c)],
            left,
            TEXT,
            arrival() if c == 1 else text_last,
        )
        for r in range(2)
        for c in range(2)
    }
    text_far_a = [
        link(txts.at[r, 3, half(0)], txts.at[r, 2, half(0)], right, TEXT, text_last)
        for r in range(2)
    ]
    text_far_b = [
        link(txts.at[r, 1, half(1)], txts.at[r, 2, half(1)], left, TEXT, text_last)
        for r in range(2)
    ]
    text_rest = link(txts.at[0], txts.at[0], right, TEXT, text_last)
    term_early = link(other_out.at[0:HOPS], other_in.at[0:HOPS], twin, TWIN)
    term_last = [
        link(other_out.at[HOPS, half(c)], other_in.at[HOPS, half(c)], twin, TWIN) for c in range(2)
    ]
    up = {
        (h, u): LoopLink(
            chain_out.at[h - 1, sliver(u)],
            chain_in.at[h - 1, sliver(u)],
            above,
            UP,
            last_z,
            relay_up.at[h - 2, u // 2] if u % 2 and h > 1 else None,
            far_above,
        )
        for h in range(1, HOPS + 1)
        for u in range(SLICES)
    }
    far_a = [link(part_out.at[r, 2, half(0)], first_a.at[r], right, PART) for r in range(2)]
    far_b = [link(part_out.at[r, 2, half(1)], first_b.at[r], left, PART) for r in range(2)]
    row_lands = [arrival() for _ in range(2)]
    near_right = {
        (r, c): link(
            part_out.at[r, 1, half(c)], second.at[r, 0, half(c)], right, PART, row_lands[r]
        )
        for r in range(2)
        for c in range(2)
    }
    near_left = {
        (r, c): link(
            part_out.at[r, 3, half(c)], second.at[r, 1, half(c)], left, PART, row_lands[r]
        )
        for r in range(2)
        for c in range(2)
    }
    near_rows = [link(second.at[r], second.at[r], right, PART, row_lands[r]) for r in range(2)]
    over_lands = arrival()
    over = [link(row_out.at[half(c)], row_in.at[half(c)], across, TEXT, over_lands) for c in range(2)]
    over_all = link(row_out, row_in, across, TEXT, over_lands)
    assert used[0] == N_ARRIVALS, used[0]

    factor = factor_ref[0]
    shift = shift_ref[0]

    @pl.when(last_z)
    def _():
        pl.semaphore_wait(barrier, 7)
        pl.semaphore_signal(go_sem, inc=1, device_id=far_above, device_id_type=MESH)

    loads[0].wait()
    inv_txt = inverse_norm(txt_ref)
    txts[0, 0] = (txt_ref[...].astype(F32) * inv_txt).astype(BF16)
    loads[1].wait()
    inv_img = inverse_norm(img_ref)
    imgs[0, 0] = (img_ref[...].astype(F32) * inv_img).astype(BF16)

    @pl.when(first_z)
    def _():
        pl.semaphore_wait(barrier, 5)

    @pl.when(jnp.logical_not(jnp.logical_or(first_z, last_z)))
    def _():
        pl.semaphore_wait(barrier, 6)

    for c in range(2):
        text_y[c].start()
        pl.when(jnp.logical_not(first_z))(down[1, c].start)
        text_right[0, c].start()
        text_left[0, c].start()
    for c in range(2):
        pl.when(first_z)(down[1, c].start)
    to_twin[0].start()

    def pass_on(h, c):
        down[h, c].wait_recv()
        if h == 1:
            pl.when(jnp.logical_not(first_z))(down[2, c].start)
        elif h < HOPS:
            down[h + 1, c].start()
        to_twin_half[h, c].start()

    def send_on(links, at_edge, *keys):
        @pl.when(at_edge)
        def _():
            for key in keys:
                links[key].send_on()

    down_on = functools.partial(send_on, down, first_z)
    up_on = functools.partial(send_on, up, last_z)

    def from_twin(h):
        to_twin[h].wait_recv()

    def spread_row(c):
        text_y[c].wait_recv()
        text_right[1, c].start()
        text_left[1, c].start()

    def coef_of(s):
        return jax.nn.sigmoid(s * factor + shift) * factor

    def scores(pictures):
        return lax.dot_general(
            pictures, txts[...].reshape(WORDS, WIDE), BOTH_LAST, preferred_element_type=F32
        )

    def coef_hops(lo, hi):
        s = scores(imgs[lo:hi].reshape((hi - lo) * 2 * ROWS, WIDE))
        coefs[lo:hi] = coef_of(s).astype(BF16).reshape(hi - lo, 2, ROWS, WORDS)
        if lo == 0:
            own = s[0:ROWS, 0:128] * factor + shift
            rows = lax.broadcasted_iota(jnp.int32, own.shape, 0)
            cols = lax.broadcasted_iota(jnp.int32, own.shape, 1)
            sign = jnp.where(rows == cols, 1.0, -1.0).astype(F32)
            value = -sign * jax.nn.sigmoid(-sign * own) * factor
            coefs[0, 0, :, 0:128] = value.astype(BF16)

    def coef_half(h, c):
        s = scores(imgs[h, :, c * HALF : (c + 1) * HALF].reshape(2 * HALF, WIDE))
        coefs[h, :, c * HALF : (c + 1) * HALF] = coef_of(s).astype(BF16).reshape(2, HALF, WORDS)

    def terms_hops(lo, hi):
        out = jnp.dot(
            coefs[lo:hi].reshape((hi - lo) * 2 * ROWS, WORDS),
            txts[...].reshape(WORDS, WIDE),
            preferred_element_type=F32,
        ).reshape(hi - lo, 2, ROWS, WIDE)
        grads[lo:hi] = out[:, 0]
        other_out[lo:hi] = out[:, 1].astype(BF16)
        term_early.start()

    def terms_half(h, c):
        out = jnp.dot(
            coefs[h, :, c * HALF : (c + 1) * HALF].reshape(2 * HALF, WORDS),
            txts[...].reshape(WORDS, WIDE),
            preferred_element_type=F32,
        ).reshape(2, HALF, WIDE)
        grads[h, half(c)] = out[0]
        other_out[h, half(c)] = out[1].astype(BF16)
        term_last[c].start()

    def climb(h, u):
        if h == HOPS and u % 2 == 0:
            term_last[u // 2].wait_recv()
        if h == HOPS - 1 and u == 0:
            term_early.wait_recv()
        total = grads[h, sliver(u)] + other_in[h, sliver(u)].astype(F32)
        if h < HOPS:
            up[h + 1, u].wait_recv()
            total = total + chain_in[h, sliver(u)].astype(F32)
        if h > 0:
            chain_out[h - 1, sliver(u)] = total.astype(BF16)
            up[h, u].start()
        else:
            grads[0, sliver(u)] = total

    spread_row(0)

    pass_on(1, 0)
    spread_row(1)
    text_right[0, 0].wait_recv()
    text_far_a[0].start()
    text_left[0, 1].wait_recv()
    text_far_b[0].start()
    pass_on(1, 1)

    @pl.when(first_z)
    def _():
        down[2, 0].start()
        pl.semaphore_wait(go_sem, 1)

    down_on((1, 0), (1, 1))
    pl.when(first_z)(down[2, 1].start)

    def far_text(side):
        (text_right[1, 0] if side == 0 else text_left[1, 1]).wait_recv()
        (text_far_a[1] if side == 0 else text_far_b[1]).start()

    pl.when(last_z)(functools.partial(far_text, 0))
    pass_on(2, 0)
    pl.when(jnp.logical_not(last_z))(functools.partial(far_text, 0))
    pl.when(last_z)(functools.partial(far_text, 1))
    pass_on(2, 1)
    pl.when(jnp.logical_not(last_z))(functools.partial(far_text, 1))

    down_on((2, 0), (2, 1))
    pass_on(3, 0)
    down_on((3, 0))
    pass_on(3, 1)
    down_on((3, 1))
    text_rest.wait_recv()
    for h in range(2):
        from_twin(h)
    coef_hops(0, 2)
    pass_on(4, 0)
    down_on((4, 0))
    for h in range(2, 4):
        from_twin(h)
    coef_hops(2, 4)
    down_on((4, 1))
    to_twin_half[4, 0].wait_recv()
    coef_half(4, 0)
    terms_half(4, 0)
    pass_on(4, 1)
    terms_hops(0, 4)
    climb(4, 0)
    climb(4, 1)

    def text_row(r):
        at = r * MINE
        total = lax.dot_general(
            coefs[:, :, :, at : at + MINE].reshape((HOPS + 1) * 2 * ROWS, MINE),
            imgs[...].reshape((HOPS + 1) * 2 * ROWS, WIDE),
            BOTH_FIRST,
            preferred_element_type=F32,
        )
        text_sum[at : at + MINE] = total
        part_out[r] = total.astype(BF16).reshape(XS, ROWS, WIDE)

    def join(r):
        far_a[r].wait_recv()
        at = (r * XS + 1) * ROWS
        part_out[r, 1, half(0)] = (text_sum[at : at + HALF] + first_a[r].astype(F32)).astype(BF16)
        near_right[r, 0].start()
        far_b[r].wait_recv()
        at = (r * XS + 3) * ROWS + HALF
        part_out[r, 3, half(1)] = (text_sum[at : at + HALF] + first_b[r].astype(F32)).astype(BF16)
        near_left[r, 1].start()

    def row_total(r):
        near_rows[r].wait_recv()
        at = r * MINE
        return (
            text_sum[at : at + ROWS]
            + second[r, 0].astype(F32)
            + second[r, 1].astype(F32)
        )

    def join_rows():
        join(1)
        near_right[0, 1].start()
        near_left[0, 0].start()

    def image_result(c):
        rows = slice(c * HALF, (c + 1) * HALF)
        img_out[rows] = back_norm(img_ref[rows], inv_img[rows], grads[0, rows])

    to_twin_half[4, 1].wait_recv()
    coef_half(4, 1)
    terms_half(4, 1)
    text_row(1)
    far_a[1].start()
    far_b[1].start()
    near_right[1, 1].start()
    near_left[1, 0].start()
    up_on((4, 1))
    climb(4, 2)
    climb(4, 3)
    text_row(0)
    far_a[0].start()
    far_b[0].start()

    def sum_row():
        row_out[...] = row_total(1).astype(BF16)
        for c in range(2):
            over[c].start()

    def own_row():
        text_sum[0:ROWS] = row_total(0)

    steps = (join_rows, functools.partial(join, 0), sum_row, own_row)

    usual = (1, 2, 3, 4)
    high = range(ZS - HOPS, ZS)
    moved = (
        {0: 0} | dict.fromkeys(high, 2),
        {0: 0, 1: 1} | dict.fromkeys(high, 3),
        {0: 1, 1: 2, 2: 2} | dict.fromkeys(high, 4),
        {0: 2, 1: 3, 2: 3, 3: 3},
    )

    def at_place(place):
        for step, common, others in zip(steps, usual, moved):
            if place == common:
                here = functools.reduce(jnp.logical_and, [z != at for at in others if others[at] != place])
                pl.when(here)(step)
            else:
                chosen = [z == at for at in others if others[at] == place]
                if chosen:
                    pl.when(functools.reduce(jnp.logical_or, chosen))(step)

    at_place(0)
    climb(3, 0)
    climb(3, 1)
    at_place(1)
    climb(3, 2)
    climb(3, 3)
    up_on((4, 3), (3, 1))
    climb(2, 0)
    climb(2, 1)
    at_place(2)
    up_on((3, 3))
    climb(2, 2)
    climb(2, 3)
    climb(1, 0)
    up_on((2, 1))
    climb(1, 1)
    at_place(3)
    up_on((2, 3))
    climb(1, 2)
    climb(1, 3)
    climb(0, 0)
    climb(0, 1)
    image_result(0)
    at_place(4)
    over_all.wait_recv()
    txt_out[...] = back_norm(txt_ref[...], inv_txt, text_sum[0:ROWS] + row_in[...].astype(F32))
    climb(0, 2)
    climb(0, 3)
    image_result(1)

    def all_left(ref, leaves):
        remote(ref, ref, twin, leaves, 0).wait_send()

    all_left(imgs, TWIN)
    all_left(txts, TEXT)
    all_left(imgs.at[0:3], PART)
    all_left(relay_down, DOWN)
    all_left(chain_out, UP)

    @pl.when(first_z)
    def _():
        all_left(relay_down, DOWN + 1)

    @pl.when(last_z)
    def _():
        all_left(relay_up, UP + 1)


N_ARRIVALS = 2 * 8 + 6 + 7 + 3 + (16 + 6) + 7


def per_device(loops, images, texts, factor, shift):
    smem = pl.BlockSpec(memory_space=pltpu.SMEM)
    hbm = pl.BlockSpec(memory_space=pltpu.HBM)
    vmem = pl.BlockSpec(memory_space=pltpu.VMEM)
    out = jax.ShapeDtypeStruct((ROWS, WIDE), F32)
    return pl.pallas_call(
        functools.partial(kernel, loops),
        out_shape=(out, out),
        in_specs=[smem, smem, hbm, hbm],
        out_specs=(vmem, vmem),
        scratch_shapes=[
            pltpu.VMEM((ROWS, WIDE), BF16),
            pltpu.VMEM((ROWS, WIDE), BF16),
            pltpu.VMEM((HOPS + 1, 2, ROWS, WIDE), BF16),
            pltpu.VMEM((2, XS, ROWS, WIDE), BF16),
            pltpu.VMEM((HOPS + 1, 2, ROWS, WORDS), BF16),
            pltpu.VMEM((HOPS + 1, ROWS, WIDE), F32),
            pltpu.VMEM((WORDS, WIDE), F32),
            pltpu.VMEM((HOPS + 1, ROWS, WIDE), BF16),
            pltpu.VMEM((HOPS + 1, ROWS, WIDE), BF16),
            pltpu.VMEM((HOPS, ROWS, WIDE), BF16),
            pltpu.VMEM((HOPS, ROWS, WIDE), BF16),
            pltpu.VMEM((2, XS, ROWS, WIDE), BF16),
            pltpu.VMEM((2, HALF, WIDE), BF16),
            pltpu.VMEM((2, HALF, WIDE), BF16),
            pltpu.VMEM((2, 2, ROWS, WIDE), BF16),
            pltpu.VMEM((ROWS, WIDE), BF16),
            pltpu.VMEM((ROWS, WIDE), BF16),
            pltpu.SemaphoreType.DMA((2,)),
            pltpu.SemaphoreType.REGULAR,
            pltpu.VMEM((HOPS, ROWS, WIDE), BF16),
            pltpu.VMEM((HOPS - 1, 2, SLICE, WIDE), BF16),
            pltpu.SemaphoreType.DMA((N_LEAVES,)),
            pltpu.SemaphoreType.DMA((N_ARRIVALS,)),
        ],
        compiler_params=pltpu.CompilerParams(
            collective_id=0, has_side_effects=True, vmem_limit_bytes=48 * 2**20
        ),
        name="siglip",
    )(
        factor,
        shift,
        pltpu.with_memory_space_constraint(images, pltpu.HBM),
        pltpu.with_memory_space_constraint(texts, pltpu.HBM),
    )


def solution(mesh):
    loops = mesh.shape["loop"]
    spec = P(("grp", "loop"), None)

    def step(images, texts, factor, shift):
        return per_device(loops, images, texts, factor, shift)

    return jax.shard_map(
        step, mesh=mesh, in_specs=(spec, spec, P(), P()), out_specs=(spec, spec), check_vma=False
    )
```

```python
import functools

import jax
import jax.numpy as jnp
from jax import lax
from jax.experimental import pallas as pl
from jax.experimental.pallas import tpu as pltpu
from jax.sharding import PartitionSpec as P

HOPS = 4
ROWS = 64
HALF = 32
SLICE = 16
SLICES = ROWS // SLICE
WIDE = 1536
XS = 4
ZS = 16
MINE = XS * ROWS
WORDS = 2 * MINE
DOWN, UP, TWIN, TEXT, PART = 0, 2, 4, 5, 6
N_LEAVES = 7
MESH = pl.DeviceIdType.MESH
F32 = jnp.float32
BF16 = jnp.bfloat16
BOTH_LAST = (((1,), (1,)), ((), ()))
BOTH_FIRST = (((0,), (0,)), ((), ()))


def half(c):
    return pl.ds(c * HALF, HALF)


def sliver(u):
    return pl.ds(u * SLICE, SLICE)


def inverse_norm(ref):
    wide = ref[...].astype(F32)
    return lax.rsqrt(jnp.sum(wide * wide, axis=-1, keepdims=True) + 1e-06)


def back_norm(raw, inverse, grad):
    unit = raw.astype(F32) * inverse
    return (grad - unit * jnp.sum(unit * grad, axis=-1, keepdims=True)) * inverse


def kernel(
    loops,
    factor_ref,
    shift_ref,
    img_hbm,
    txt_hbm,
    both_out,
    img_ref,
    txt_ref,
    imgs,
    txts,
    coefs,
    grads,
    text_sum,
    other_out,
    other_in,
    chain_out,
    chain_in,
    part_out,
    first_a,
    first_b,
    second,
    row_out,
    row_in,
    load_sem,
    go_sem,
    relay_down,
    relay_up,
    send_sem,
    recv_sem,
):
    g = lax.axis_index("grp")
    q = lax.axis_index("loop")
    x = g // 4
    y = (g // 2) % 2
    core = g % 2
    z = q % ZS

    def member(xx, yy, cc):
        return {"grp": xx * 4 + yy * 2 + cc, "loop": q}

    twin = member(x, y, 1 - core)
    across = member(x, 1 - y, core)
    right = member((x + 1) % XS, y, core)
    left = member((x + XS - 1) % XS, y, core)
    below = {"grp": g, "loop": (q + loops - 1) % loops}
    above = {"grp": g, "loop": (q + 1) % loops}
    first_z = z == 0
    last_z = z == ZS - 1
    far_below = {"grp": across["grp"], "loop": below["loop"]}
    far_above = {"grp": across["grp"], "loop": above["loop"]}

    loads = [
        pltpu.make_async_copy(txt_hbm, txt_ref, load_sem.at[0]),
        pltpu.make_async_copy(img_hbm, img_ref, load_sem.at[1]),
    ]
    for load in loads:
        load.start()

    barrier = pltpu.get_barrier_semaphore()
    for peer in (twin, across, right, left):
        pl.semaphore_signal(barrier, inc=1, device_id=peer, device_id_type=MESH)

    @pl.when(first_z)
    def _():
        pl.semaphore_signal(barrier, inc=1, device_id=far_below, device_id_type=MESH)

    pl.semaphore_signal(barrier, inc=1, device_id=below, device_id_type=MESH)

    @pl.when(jnp.logical_not(last_z))
    def _():
        pl.semaphore_signal(barrier, inc=1, device_id=above, device_id_type=MESH)

    used = [0]

    def arrival():
        used[0] += 1
        return used[0] - 1

    def remote(src, dst, device, leaves, lands):
        return pltpu.make_async_remote_copy(
            src_ref=src,
            dst_ref=dst,
            send_sem=send_sem.at[leaves],
            recv_sem=recv_sem.at[lands],
            device_id=device,
            device_id_type=MESH,
        )

    def link(src, dst, device, leaves, lands=None):
        return remote(src, dst, device, leaves, arrival() if lands is None else lands)

    class LoopLink:
        def __init__(self, src, dst, device, leaves, at_edge, relay, onto):
            self.at_edge, self.relay = at_edge, relay
            lands = arrival()
            self.plain = remote(src, dst, device, leaves, lands)
            if relay is not None:
                self.aside = remote(src, relay, across, leaves, arrival())
                self.onward = remote(relay, dst, onto, leaves + 1, lands)

        def start(self):
            if self.relay is None:
                self.plain.start()
            else:
                pl.when(jnp.logical_not(self.at_edge))(self.plain.start)
                pl.when(self.at_edge)(self.aside.start)

        def send_on(self):
            self.aside.wait_recv()
            self.onward.start()

        def wait_recv(self):
            self.plain.wait_recv()

    down = {
        (h, c): LoopLink(
            imgs.at[h - 1, 0, half(c)],
            imgs.at[h, 0, half(c)],
            below,
            DOWN,
            first_z,
            relay_down.at[h - 1, half(c)],
            far_below,
        )
        for h in range(1, HOPS + 1)
        for c in range(2)
    }
    to_twin = [link(imgs.at[0, 0], imgs.at[0, 1], twin, TWIN)]
    to_twin_half = {}
    for h in range(1, HOPS + 1):
        lands = arrival()
        for c in range(2):
            alone = lands if h < HOPS or c == 0 else arrival()
            to_twin_half[h, c] = link(
                imgs.at[h, 0, half(c)], imgs.at[h, 1, half(c)], twin, TWIN, alone
            )
        if h < HOPS:
            to_twin.append(link(imgs.at[h, 0], imgs.at[h, 1], twin, TWIN, lands))
    text_y = [
        link(txts.at[0, 0, half(c)], txts.at[1, 0, half(c)], across, TEXT) for c in range(2)
    ]
    text_last = arrival()
    text_right = {
        (r, c): link(
            txts.at[r, 0, half(c)],
            txts.at[r, 3, half(c)],
            right,
            TEXT,
            arrival() if c == 0 else text_last,
        )
        for r in range(2)
        for c in range(2)
    }
    text_left = {
        (r, c): link(
            txts.at[r, 0, half(c)],
            txts.at[r, 1, half(c)],
            left,
            TEXT,
            arrival() if c == 1 else text_last,
        )
        for r in range(2)
        for c in range(2)
    }
    text_far_a = [
        link(txts.at[r, 3, half(0)], txts.at[r, 2, half(0)], right, TEXT, text_last)
        for r in range(2)
    ]
    text_far_b = [
        link(txts.at[r, 1, half(1)], txts.at[r, 2, half(1)], left, TEXT, text_last)
        for r in range(2)
    ]
    text_rest = link(txts.at[0], txts.at[0], right, TEXT, text_last)
    term_early = link(other_out.at[0:HOPS], other_in.at[0:HOPS], twin, TWIN)
    term_last = [
        link(other_out.at[HOPS, half(c)], other_in.at[HOPS, half(c)], twin, TWIN) for c in range(2)
    ]
    up = {
        (h, u): LoopLink(
            chain_out.at[h - 1, sliver(u)],
            chain_in.at[h - 1, sliver(u)],
            above,
            UP,
            last_z,
            relay_up.at[h - 3, u // 2] if u % 2 and h > 2 else None,
            far_above,
        )
        for h in range(1, HOPS + 1)
        for u in range(SLICES)
    }
    far_a = [link(part_out.at[r, 2, half(0)], first_a.at[r], right, PART) for r in range(2)]
    far_b = [link(part_out.at[r, 2, half(1)], first_b.at[r], left, PART) for r in range(2)]
    row_lands = [arrival() for _ in range(2)]
    near_right = {
        (r, c): link(
            part_out.at[r, 1, half(c)], second.at[r, 0, half(c)], right, PART, row_lands[r]
        )
        for r in range(2)
        for c in range(2)
    }
    near_left = {
        (r, c): link(
            part_out.at[r, 3, half(c)], second.at[r, 1, half(c)], left, PART, row_lands[r]
        )
        for r in range(2)
        for c in range(2)
    }
    near_rows = [link(second.at[r], second.at[r], right, PART, row_lands[r]) for r in range(2)]
    over_lands = arrival()
    over = [link(row_out.at[half(c)], row_in.at[half(c)], across, TEXT, over_lands) for c in range(2)]
    over_all = link(row_out, row_in, across, TEXT, over_lands)
    assert used[0] == N_ARRIVALS, used[0]

    factor = factor_ref[0]
    shift = shift_ref[0]

    @pl.when(last_z)
    def _():
        pl.semaphore_wait(barrier, 7)
        pl.semaphore_signal(go_sem, inc=1, device_id=far_above, device_id_type=MESH)

    loads[0].wait()
    inv_txt = inverse_norm(txt_ref)
    txts[0, 0] = (txt_ref[...].astype(F32) * inv_txt).astype(BF16)
    loads[1].wait()
    inv_img = inverse_norm(img_ref)
    imgs[0, 0] = (img_ref[...].astype(F32) * inv_img).astype(BF16)

    @pl.when(first_z)
    def _():
        pl.semaphore_wait(barrier, 5)

    @pl.when(jnp.logical_not(jnp.logical_or(first_z, last_z)))
    def _():
        pl.semaphore_wait(barrier, 6)

    for c in range(2):
        text_y[c].start()
        pl.when(jnp.logical_not(first_z))(down[1, c].start)
        text_right[0, c].start()
        text_left[0, c].start()
    for c in range(2):
        pl.when(first_z)(down[1, c].start)
    to_twin[0].start()

    def pass_on(h, c):
        down[h, c].wait_recv()
        if h == 1:
            pl.when(jnp.logical_not(first_z))(down[2, c].start)
        elif h < HOPS:
            down[h + 1, c].start()
        to_twin_half[h, c].start()

    def send_on(links, at_edge, *keys):
        @pl.when(at_edge)
        def _():
            for key in keys:
                links[key].send_on()

    down_on = functools.partial(send_on, down, first_z)
    up_on = functools.partial(send_on, up, last_z)

    def from_twin(h):
        to_twin[h].wait_recv()

    def spread_row(c):
        text_y[c].wait_recv()
        text_right[1, c].start()
        text_left[1, c].start()

    def coef_of(s):
        return jax.nn.sigmoid(s * factor + shift) * factor

    def scores(pictures):
        return lax.dot_general(
            pictures, txts[...].reshape(WORDS, WIDE), BOTH_LAST, preferred_element_type=F32
        )

    def coef_hops(lo, hi):
        s = scores(imgs[lo:hi].reshape((hi - lo) * 2 * ROWS, WIDE))
        coefs[lo:hi] = coef_of(s).astype(BF16).reshape(hi - lo, 2, ROWS, WORDS)
        if lo == 0:
            own = s[0:ROWS, 0:128] * factor + shift
            rows = lax.broadcasted_iota(jnp.int32, own.shape, 0)
            cols = lax.broadcasted_iota(jnp.int32, own.shape, 1)
            sign = jnp.where(rows == cols, 1.0, -1.0).astype(F32)
            value = -sign * jax.nn.sigmoid(-sign * own) * factor
            coefs[0, 0, :, 0:128] = value.astype(BF16)

    def coef_half(h, c):
        s = scores(imgs[h, :, c * HALF : (c + 1) * HALF].reshape(2 * HALF, WIDE))
        coefs[h, :, c * HALF : (c + 1) * HALF] = coef_of(s).astype(BF16).reshape(2, HALF, WORDS)

    def terms_hops(lo, hi):
        out = jnp.dot(
            coefs[lo:hi].reshape((hi - lo) * 2 * ROWS, WORDS),
            txts[...].reshape(WORDS, WIDE),
            preferred_element_type=F32,
        ).reshape(hi - lo, 2, ROWS, WIDE)
        grads[lo:hi] = out[:, 0]
        other_out[lo:hi] = out[:, 1].astype(BF16)
        term_early.start()

    def terms_half(h, c):
        out = jnp.dot(
            coefs[h, :, c * HALF : (c + 1) * HALF].reshape(2 * HALF, WORDS),
            txts[...].reshape(WORDS, WIDE),
            preferred_element_type=F32,
        ).reshape(2, HALF, WIDE)
        grads[h, half(c)] = out[0]
        other_out[h, half(c)] = out[1].astype(BF16)
        term_last[c].start()

    def climb(h, u):
        if h == HOPS and u % 2 == 0:
            term_last[u // 2].wait_recv()
        if h == HOPS - 1 and u == 0:
            term_early.wait_recv()
        total = grads[h, sliver(u)] + other_in[h, sliver(u)].astype(F32)
        if h < HOPS:
            up[h + 1, u].wait_recv()
            total = total + chain_in[h, sliver(u)].astype(F32)
        if h > 0:
            chain_out[h - 1, sliver(u)] = total.astype(BF16)
            up[h, u].start()
        else:
            grads[0, sliver(u)] = total

    spread_row(0)

    pass_on(1, 0)
    spread_row(1)
    text_right[0, 0].wait_recv()
    text_far_a[0].start()
    text_left[0, 1].wait_recv()
    text_far_b[0].start()
    pass_on(1, 1)

    @pl.when(first_z)
    def _():
        down[2, 0].start()
        pl.semaphore_wait(go_sem, 1)

    down_on((1, 0), (1, 1))
    pl.when(first_z)(down[2, 1].start)

    def far_text(side):
        (text_right[1, 0] if side == 0 else text_left[1, 1]).wait_recv()
        (text_far_a[1] if side == 0 else text_far_b[1]).start()

    pl.when(last_z)(functools.partial(far_text, 0))
    pass_on(2, 0)
    pl.when(jnp.logical_not(last_z))(functools.partial(far_text, 0))
    pl.when(last_z)(functools.partial(far_text, 1))
    pass_on(2, 1)
    pl.when(jnp.logical_not(last_z))(functools.partial(far_text, 1))

    down_on((2, 0), (2, 1))
    pass_on(3, 0)
    down_on((3, 0))
    pass_on(3, 1)
    down_on((3, 1))
    text_rest.wait_recv()
    for h in range(2):
        from_twin(h)
    coef_hops(0, 2)
    pass_on(4, 0)
    down_on((4, 0))
    for h in range(2, 4):
        from_twin(h)
    coef_hops(2, 4)
    down_on((4, 1))
    to_twin_half[4, 0].wait_recv()
    coef_half(4, 0)
    terms_half(4, 0)
    pass_on(4, 1)
    terms_hops(0, 4)
    climb(4, 0)
    climb(4, 1)

    def text_row(r):
        at = r * MINE
        total = lax.dot_general(
            coefs[:, :, :, at : at + MINE].reshape((HOPS + 1) * 2 * ROWS, MINE),
            imgs[...].reshape((HOPS + 1) * 2 * ROWS, WIDE),
            BOTH_FIRST,
            preferred_element_type=F32,
        )
        text_sum[at : at + MINE] = total
        part_out[r] = total.astype(BF16).reshape(XS, ROWS, WIDE)

    def join(r):
        far_a[r].wait_recv()
        at = (r * XS + 1) * ROWS
        part_out[r, 1, half(0)] = (text_sum[at : at + HALF] + first_a[r].astype(F32)).astype(BF16)
        near_right[r, 0].start()
        far_b[r].wait_recv()
        at = (r * XS + 3) * ROWS + HALF
        part_out[r, 3, half(1)] = (text_sum[at : at + HALF] + first_b[r].astype(F32)).astype(BF16)
        near_left[r, 1].start()

    def row_total(r):
        near_rows[r].wait_recv()
        at = r * MINE
        return (
            text_sum[at : at + ROWS]
            + second[r, 0].astype(F32)
            + second[r, 1].astype(F32)
        )

    def join_rows():
        join(1)
        near_right[0, 1].start()
        near_left[0, 0].start()

    def image_result(c):
        rows = slice(c * HALF, (c + 1) * HALF)
        both_out[0, rows] = back_norm(img_ref[rows], inv_img[rows], grads[0, rows])

    to_twin_half[4, 1].wait_recv()
    coef_half(4, 1)
    terms_half(4, 1)
    text_row(1)
    far_a[1].start()
    far_b[1].start()
    near_right[1, 1].start()
    near_left[1, 0].start()
    up_on((4, 1))
    climb(4, 2)
    climb(4, 3)
    text_row(0)
    far_a[0].start()
    far_b[0].start()

    def sum_row():
        row_out[...] = row_total(1).astype(BF16)
        for c in range(2):
            over[c].start()

    def own_row():
        text_sum[0:ROWS] = row_total(0)

    steps = (join_rows, functools.partial(join, 0), sum_row, own_row)

    usual = (1, 2, 3, 4)
    high = range(ZS - HOPS, ZS)
    moved = (
        {0: 0} | dict.fromkeys(high, 2),
        {0: 0, 1: 1} | dict.fromkeys(high, 3),
        {0: 1, 1: 2, 2: 2} | dict.fromkeys(high, 4),
        {0: 2, 1: 3, 2: 3, 3: 3},
    )

    def at_place(place):
        for step, common, others in zip(steps, usual, moved):
            if place == common:
                here = functools.reduce(jnp.logical_and, [z != at for at in others if others[at] != place])
                pl.when(here)(step)
            else:
                chosen = [z == at for at in others if others[at] == place]
                if chosen:
                    pl.when(functools.reduce(jnp.logical_or, chosen))(step)

    at_place(0)
    climb(3, 0)
    climb(3, 1)
    at_place(1)
    climb(3, 2)
    climb(3, 3)
    up_on((4, 3), (3, 1))
    climb(2, 0)
    climb(2, 1)
    at_place(2)
    up_on((3, 3))
    climb(2, 2)
    climb(2, 3)
    climb(1, 0)
    climb(1, 1)
    at_place(3)
    climb(1, 2)
    climb(1, 3)
    climb(0, 0)
    climb(0, 1)
    image_result(0)
    at_place(4)
    over_all.wait_recv()
    both_out[1] = back_norm(txt_ref[...], inv_txt, text_sum[0:ROWS] + row_in[...].astype(F32))
    climb(0, 2)
    climb(0, 3)
    image_result(1)

    def all_left(ref, leaves):
        remote(ref, ref, twin, leaves, 0).wait_send()

    all_left(imgs, TWIN)
    all_left(txts, TEXT)
    all_left(imgs.at[0:3], PART)
    all_left(relay_down, DOWN)
    all_left(chain_out, UP)

    @pl.when(first_z)
    def _():
        all_left(relay_down, DOWN + 1)

    @pl.when(last_z)
    def _():
        all_left(relay_up, UP + 1)


N_ARRIVALS = 2 * 8 + 6 + 7 + 3 + (16 + 4) + 7


def per_device(loops, images, texts, factor, shift):
    smem = pl.BlockSpec(memory_space=pltpu.SMEM)
    hbm = pl.BlockSpec(memory_space=pltpu.HBM)
    vmem = pl.BlockSpec(memory_space=pltpu.VMEM)
    out = jax.ShapeDtypeStruct((2, ROWS, WIDE), F32)
    both = pl.pallas_call(
        functools.partial(kernel, loops),
        out_shape=out,
        in_specs=[smem, smem, hbm, hbm],
        out_specs=vmem,
        scratch_shapes=[
            pltpu.VMEM((ROWS, WIDE), BF16),
            pltpu.VMEM((ROWS, WIDE), BF16),
            pltpu.VMEM((HOPS + 1, 2, ROWS, WIDE), BF16),
            pltpu.VMEM((2, XS, ROWS, WIDE), BF16),
            pltpu.VMEM((HOPS + 1, 2, ROWS, WORDS), BF16),
            pltpu.VMEM((HOPS + 1, ROWS, WIDE), F32),
            pltpu.VMEM((WORDS, WIDE), F32),
            pltpu.VMEM((HOPS + 1, ROWS, WIDE), BF16),
            pltpu.VMEM((HOPS + 1, ROWS, WIDE), BF16),
            pltpu.VMEM((HOPS, ROWS, WIDE), BF16),
            pltpu.VMEM((HOPS, ROWS, WIDE), BF16),
            pltpu.VMEM((2, XS, ROWS, WIDE), BF16),
            pltpu.VMEM((2, HALF, WIDE), BF16),
            pltpu.VMEM((2, HALF, WIDE), BF16),
            pltpu.VMEM((2, 2, ROWS, WIDE), BF16),
            pltpu.VMEM((ROWS, WIDE), BF16),
            pltpu.VMEM((ROWS, WIDE), BF16),
            pltpu.SemaphoreType.DMA((2,)),
            pltpu.SemaphoreType.REGULAR,
            pltpu.VMEM((HOPS, ROWS, WIDE), BF16),
            pltpu.VMEM((HOPS - 2, 2, SLICE, WIDE), BF16),
            pltpu.SemaphoreType.DMA((N_LEAVES,)),
            pltpu.SemaphoreType.DMA((N_ARRIVALS,)),
        ],
        compiler_params=pltpu.CompilerParams(
            collective_id=0, has_side_effects=True, vmem_limit_bytes=48 * 2**20
        ),
        name="siglip",
    )(
        factor,
        shift,
        pltpu.with_memory_space_constraint(images, pltpu.HBM),
        pltpu.with_memory_space_constraint(texts, pltpu.HBM),
    )
    return both[0], both[1]


def solution(mesh):
    loops = mesh.shape["loop"]
    spec = P(("grp", "loop"), None)

    def step(images, texts, factor, shift):
        return per_device(loops, images, texts, factor, shift)

    return jax.shard_map(
        step, mesh=mesh, in_specs=(spec, spec, P(), P()), out_specs=(spec, spec), check_vma=False
    )
```

```python
import functools

import jax
import jax.numpy as jnp
from jax import lax
from jax.experimental import pallas as pl
from jax.experimental.pallas import tpu as pltpu
from jax.sharding import PartitionSpec as P

HOPS = 4
ROWS = 64
HALF = 32
SLICE = 16
SLICES = ROWS // SLICE
WIDE = 1536
XS = 4
ZS = 16
MINE = XS * ROWS
WORDS = 2 * MINE
DOWN, UP, TWIN, TEXT, PART = 0, 2, 4, 5, 6
N_LEAVES = 7
ROUND = ((4, 3), (3, 1), (3, 3), (2, 1))
MESH = pl.DeviceIdType.MESH
F32 = jnp.float32
BF16 = jnp.bfloat16
BOTH_LAST = (((1,), (1,)), ((), ()))
BOTH_FIRST = (((0,), (0,)), ((), ()))


def half(c):
    return pl.ds(c * HALF, HALF)


def sliver(u):
    return pl.ds(u * SLICE, SLICE)


def inverse_norm(ref):
    wide = ref[...].astype(F32)
    return lax.rsqrt(jnp.sum(wide * wide, axis=-1, keepdims=True) + 1e-06)


def back_norm(raw, inverse, grad):
    unit = raw.astype(F32) * inverse
    return (grad - unit * jnp.sum(unit * grad, axis=-1, keepdims=True)) * inverse


def kernel(
    loops,
    factor_ref,
    shift_ref,
    img_hbm,
    txt_hbm,
    both_out,
    img_ref,
    txt_ref,
    imgs,
    txts,
    coefs,
    grads,
    text_sum,
    other_out,
    other_in,
    chain_out,
    chain_in,
    part_out,
    first_a,
    first_b,
    second,
    row_out,
    row_in,
    load_sem,
    go_sem,
    relay_down,
    relay_up,
    send_sem,
    recv_sem,
):
    g = lax.axis_index("grp")
    q = lax.axis_index("loop")
    x = g // 4
    y = (g // 2) % 2
    core = g % 2
    z = q % ZS

    def member(xx, yy, cc):
        return {"grp": xx * 4 + yy * 2 + cc, "loop": q}

    twin = member(x, y, 1 - core)
    across = member(x, 1 - y, core)
    right = member((x + 1) % XS, y, core)
    left = member((x + XS - 1) % XS, y, core)
    below = {"grp": g, "loop": (q + loops - 1) % loops}
    above = {"grp": g, "loop": (q + 1) % loops}
    first_z = z == 0
    last_z = z == ZS - 1
    far_below = {"grp": across["grp"], "loop": below["loop"]}
    far_above = {"grp": across["grp"], "loop": above["loop"]}

    loads = [
        pltpu.make_async_copy(txt_hbm, txt_ref, load_sem.at[0]),
        pltpu.make_async_copy(img_hbm, img_ref, load_sem.at[1]),
    ]
    for load in loads:
        load.start()

    barrier = pltpu.get_barrier_semaphore()
    for peer in (twin, across, right, left):
        pl.semaphore_signal(barrier, inc=1, device_id=peer, device_id_type=MESH)

    @pl.when(first_z)
    def _():
        pl.semaphore_signal(barrier, inc=1, device_id=far_below, device_id_type=MESH)

    pl.semaphore_signal(barrier, inc=1, device_id=below, device_id_type=MESH)

    @pl.when(jnp.logical_not(last_z))
    def _():
        pl.semaphore_signal(barrier, inc=1, device_id=above, device_id_type=MESH)

    used = [0]

    def arrival():
        used[0] += 1
        return used[0] - 1

    def remote(src, dst, device, leaves, lands):
        return pltpu.make_async_remote_copy(
            src_ref=src,
            dst_ref=dst,
            send_sem=send_sem.at[leaves],
            recv_sem=recv_sem.at[lands],
            device_id=device,
            device_id_type=MESH,
        )

    def link(src, dst, device, leaves, lands=None):
        return remote(src, dst, device, leaves, arrival() if lands is None else lands)

    class LoopLink:
        def __init__(self, src, dst, device, leaves, at_edge, relay, onto):
            self.at_edge, self.relay = at_edge, relay
            lands = arrival()
            self.plain = remote(src, dst, device, leaves, lands)
            if relay is not None:
                self.aside = remote(src, relay, across, leaves, arrival())
                self.onward = remote(relay, dst, onto, leaves + 1, lands)

        def start(self):
            if self.relay is None:
                self.plain.start()
            else:
                pl.when(jnp.logical_not(self.at_edge))(self.plain.start)
                pl.when(self.at_edge)(self.aside.start)

        def send_on(self):
            self.aside.wait_recv()
            self.onward.start()

        def wait_recv(self):
            self.plain.wait_recv()

    down = {
        (h, u): LoopLink(
            imgs.at[h - 1, 0, sliver(u)],
            imgs.at[h, 0, sliver(u)],
            below,
            DOWN,
            first_z,
            relay_down.at[h - 1, sliver(u)],
            far_below,
        )
        for h in range(1, HOPS + 1)
        for u in range(SLICES)
    }
    to_twin = [link(imgs.at[0, 0], imgs.at[0, 1], twin, TWIN)]
    to_twin_half = {}
    for h in range(1, HOPS + 1):
        lands = arrival()
        for c in range(2):
            alone = lands if h < HOPS or c == 0 else arrival()
            to_twin_half[h, c] = link(
                imgs.at[h, 0, half(c)], imgs.at[h, 1, half(c)], twin, TWIN, alone
            )
        if h < HOPS:
            to_twin.append(link(imgs.at[h, 0], imgs.at[h, 1], twin, TWIN, lands))
    text_y = [
        link(txts.at[0, 0, half(c)], txts.at[1, 0, half(c)], across, TEXT) for c in range(2)
    ]
    text_last = arrival()
    text_right = {
        (r, c): link(
            txts.at[r, 0, half(c)],
            txts.at[r, 3, half(c)],
            right,
            TEXT,
            arrival() if c == 0 else text_last,
        )
        for r in range(2)
        for c in range(2)
    }
    text_left = {
        (r, c): link(
            txts.at[r, 0, half(c)],
            txts.at[r, 1, half(c)],
            left,
            TEXT,
            arrival() if c == 1 else text_last,
        )
        for r in range(2)
        for c in range(2)
    }
    text_far_a = [
        link(txts.at[r, 3, half(0)], txts.at[r, 2, half(0)], right, TEXT, text_last)
        for r in range(2)
    ]
    text_far_b = [
        link(txts.at[r, 1, half(1)], txts.at[r, 2, half(1)], left, TEXT, text_last)
        for r in range(2)
    ]
    text_rest = link(txts.at[0], txts.at[0], right, TEXT, text_last)
    term_early = link(other_out.at[0:HOPS], other_in.at[0:HOPS], twin, TWIN)
    term_last = [
        link(other_out.at[HOPS, half(c)], other_in.at[HOPS, half(c)], twin, TWIN) for c in range(2)
    ]
    up = {
        (h, u): LoopLink(
            chain_out.at[h - 1, sliver(u)],
            chain_in.at[h - 1, sliver(u)],
            above,
            UP,
            last_z,
            relay_up.at[ROUND.index((h, u))] if (h, u) in ROUND else None,
            far_above,
        )
        for h in range(1, HOPS + 1)
        for u in range(SLICES)
    }
    far_a = [link(part_out.at[r, 2, half(0)], first_a.at[r], right, PART) for r in range(2)]
    far_b = [link(part_out.at[r, 2, half(1)], first_b.at[r], left, PART) for r in range(2)]
    row_lands = [arrival() for _ in range(2)]
    near_right = {
        (r, c): link(
            part_out.at[r, 1, half(c)], second.at[r, 0, half(c)], right, PART, row_lands[r]
        )
        for r in range(2)
        for c in range(2)
    }
    near_left = {
        (r, c): link(
            part_out.at[r, 3, half(c)], second.at[r, 1, half(c)], left, PART, row_lands[r]
        )
        for r in range(2)
        for c in range(2)
    }
    near_rows = [link(second.at[r], second.at[r], right, PART, row_lands[r]) for r in range(2)]
    over_lands = arrival()
    over = [link(row_out.at[half(c)], row_in.at[half(c)], across, TEXT, over_lands) for c in range(2)]
    over_all = link(row_out, row_in, across, TEXT, over_lands)
    assert used[0] == N_ARRIVALS, used[0]

    factor = factor_ref[0]
    shift = shift_ref[0]

    @pl.when(last_z)
    def _():
        pl.semaphore_wait(barrier, 7)
        pl.semaphore_signal(go_sem, inc=1, device_id=far_above, device_id_type=MESH)

    loads[0].wait()
    inv_txt = inverse_norm(txt_ref)
    txts[0, 0] = (txt_ref[...].astype(F32) * inv_txt).astype(BF16)
    loads[1].wait()
    inv_img = inverse_norm(img_ref)
    imgs[0, 0] = (img_ref[...].astype(F32) * inv_img).astype(BF16)

    @pl.when(first_z)
    def _():
        pl.semaphore_wait(barrier, 5)

    @pl.when(jnp.logical_not(jnp.logical_or(first_z, last_z)))
    def _():
        pl.semaphore_wait(barrier, 6)

    for c in range(2):
        text_y[c].start()
        for u in (2 * c, 2 * c + 1):
            pl.when(jnp.logical_not(first_z))(down[1, u].start)
        text_right[0, c].start()
        text_left[0, c].start()
    for u in range(SLICES):
        pl.when(first_z)(down[1, u].start)
    to_twin[0].start()

    def pass_on(h, *slivers):
        for u in slivers:
            down[h, u].wait_recv()
            if h == 1:
                pl.when(jnp.logical_not(first_z))(down[2, u].start)
            elif h < HOPS:
                down[h + 1, u].start()
            if u % 2:
                to_twin_half[h, u // 2].start()

    def send_on(links, at_edge, *keys):
        @pl.when(at_edge)
        def _():
            for key in keys:
                links[key].send_on()

    down_on = functools.partial(send_on, down, first_z)
    up_on = functools.partial(send_on, up, last_z)

    def from_twin(h):
        to_twin[h].wait_recv()

    def spread_row(c):
        text_y[c].wait_recv()
        text_right[1, c].start()
        text_left[1, c].start()

    def coef_of(s):
        return jax.nn.sigmoid(s * factor + shift) * factor

    def scores(pictures):
        return lax.dot_general(
            pictures, txts[...].reshape(WORDS, WIDE), BOTH_LAST, preferred_element_type=F32
        )

    def coef_hops(lo, hi):
        s = scores(imgs[lo:hi].reshape((hi - lo) * 2 * ROWS, WIDE))
        coefs[lo:hi] = coef_of(s).astype(BF16).reshape(hi - lo, 2, ROWS, WORDS)
        if lo == 0:
            own = s[0:ROWS, 0:128] * factor + shift
            rows = lax.broadcasted_iota(jnp.int32, own.shape, 0)
            cols = lax.broadcasted_iota(jnp.int32, own.shape, 1)
            sign = jnp.where(rows == cols, 1.0, -1.0).astype(F32)
            value = -sign * jax.nn.sigmoid(-sign * own) * factor
            coefs[0, 0, :, 0:128] = value.astype(BF16)

    def coef_half(h, c):
        s = scores(imgs[h, :, c * HALF : (c + 1) * HALF].reshape(2 * HALF, WIDE))
        coefs[h, :, c * HALF : (c + 1) * HALF] = coef_of(s).astype(BF16).reshape(2, HALF, WORDS)

    def terms_hops(lo, hi):
        out = jnp.dot(
            coefs[lo:hi].reshape((hi - lo) * 2 * ROWS, WORDS),
            txts[...].reshape(WORDS, WIDE),
            preferred_element_type=F32,
        ).reshape(hi - lo, 2, ROWS, WIDE)
        grads[lo:hi] = out[:, 0]
        other_out[lo:hi] = out[:, 1].astype(BF16)
        term_early.start()

    def terms_half(h, c):
        out = jnp.dot(
            coefs[h, :, c * HALF : (c + 1) * HALF].reshape(2 * HALF, WORDS),
            txts[...].reshape(WORDS, WIDE),
            preferred_element_type=F32,
        ).reshape(2, HALF, WIDE)
        grads[h, half(c)] = out[0]
        other_out[h, half(c)] = out[1].astype(BF16)
        term_last[c].start()

    def climb(h, u):
        if h == HOPS and u % 2 == 0:
            term_last[u // 2].wait_recv()
        if h == HOPS - 1 and u == 0:
            term_early.wait_recv()
        total = grads[h, sliver(u)] + other_in[h, sliver(u)].astype(F32)
        if h < HOPS:
            up[h + 1, u].wait_recv()
            total = total + chain_in[h, sliver(u)].astype(F32)
        if h > 0:
            chain_out[h - 1, sliver(u)] = total.astype(BF16)
            up[h, u].start()
        else:
            grads[0, sliver(u)] = total

    def far_text(side):
        (text_right[1, 0] if side == 0 else text_left[1, 1]).wait_recv()
        (text_far_a[1] if side == 0 else text_far_b[1]).start()

    not_last = jnp.logical_not(last_z)
    pl.when(not_last)(functools.partial(pass_on, 1, 0))
    spread_row(0)
    pl.when(last_z)(functools.partial(pass_on, 1, 0))
    pass_on(1, 1, 2)
    spread_row(1)
    text_right[0, 0].wait_recv()
    text_far_a[0].start()
    pass_on(1, 3)
    text_left[0, 1].wait_recv()
    text_far_b[0].start()

    @pl.when(first_z)
    def _():
        down[2, 0].start()
        down[2, 1].start()
        pl.semaphore_wait(go_sem, 1)

    down_on((1, 0), (1, 1), (1, 2), (1, 3))
    for u in (2, 3):
        pl.when(first_z)(down[2, u].start)
    pl.when(last_z)(functools.partial(far_text, 0))
    pass_on(2, 0, 1)
    pl.when(not_last)(functools.partial(far_text, 0))
    pl.when(last_z)(functools.partial(far_text, 1))
    pass_on(2, 2, 3)
    pl.when(not_last)(functools.partial(far_text, 1))
    down_on((2, 0), (2, 1))
    pass_on(3, 0)
    down_on((2, 2), (2, 3))
    pass_on(3, 1)
    down_on((3, 0))
    pass_on(3, 2)
    down_on((3, 1))
    pass_on(3, 3)
    down_on((3, 2))
    text_rest.wait_recv()
    down_on((3, 3))
    for h in range(2):
        from_twin(h)
    coef_hops(0, 2)
    pass_on(4, 0, 1)
    down_on((4, 0), (4, 1))
    for h in range(2, 4):
        from_twin(h)
    coef_hops(2, 4)
    down_on((4, 2), (4, 3))
    to_twin_half[4, 0].wait_recv()
    coef_half(4, 0)
    terms_half(4, 0)
    pass_on(4, 2, 3)
    terms_hops(0, 4)
    climb(4, 0)
    climb(4, 1)

    def text_row(r):
        at = r * MINE
        total = lax.dot_general(
            coefs[:, :, :, at : at + MINE].reshape((HOPS + 1) * 2 * ROWS, MINE),
            imgs[...].reshape((HOPS + 1) * 2 * ROWS, WIDE),
            BOTH_FIRST,
            preferred_element_type=F32,
        )
        text_sum[at : at + MINE] = total
        part_out[r] = total.astype(BF16).reshape(XS, ROWS, WIDE)

    def join(r):
        far_a[r].wait_recv()
        at = (r * XS + 1) * ROWS
        part_out[r, 1, half(0)] = (text_sum[at : at + HALF] + first_a[r].astype(F32)).astype(BF16)
        near_right[r, 0].start()
        far_b[r].wait_recv()
        at = (r * XS + 3) * ROWS + HALF
        part_out[r, 3, half(1)] = (text_sum[at : at + HALF] + first_b[r].astype(F32)).astype(BF16)
        near_left[r, 1].start()

    def row_total(r):
        near_rows[r].wait_recv()
        at = r * MINE
        return (
            text_sum[at : at + ROWS]
            + second[r, 0].astype(F32)
            + second[r, 1].astype(F32)
        )

    def join_rows():
        join(1)
        near_right[0, 1].start()
        near_left[0, 0].start()

    def image_result(c):
        rows = slice(c * HALF, (c + 1) * HALF)
        both_out[0, rows] = back_norm(img_ref[rows], inv_img[rows], grads[0, rows])

    to_twin_half[4, 1].wait_recv()
    coef_half(4, 1)
    terms_half(4, 1)
    text_row(1)
    far_a[1].start()
    far_b[1].start()
    near_right[1, 1].start()
    near_left[1, 0].start()
    climb(4, 2)
    climb(4, 3)
    text_row(0)
    far_a[0].start()
    far_b[0].start()

    def sum_row():
        row_out[...] = row_total(1).astype(BF16)
        for c in range(2):
            over[c].start()

    def own_row():
        text_sum[0:ROWS] = row_total(0)

    steps = (join_rows, functools.partial(join, 0), sum_row, own_row)

    usual = (1, 2, 3, 4)
    high = range(ZS - HOPS, ZS)
    moved = (
        {0: 0} | dict.fromkeys(high, 2),
        {0: 0, 1: 1} | dict.fromkeys(high, 3),
        {0: 1, 1: 2, 2: 2} | dict.fromkeys(high, 4),
        {0: 2, 1: 3, 2: 3, 3: 3},
    )

    def at_place(place):
        for step, common, others in zip(steps, usual, moved):
            if place == common:
                here = functools.reduce(jnp.logical_and, [z != at for at in others if others[at] != place])
                pl.when(here)(step)
            else:
                chosen = [z == at for at in others if others[at] == place]
                if chosen:
                    pl.when(functools.reduce(jnp.logical_or, chosen))(step)

    at_place(0)
    climb(3, 0)
    climb(3, 1)
    at_place(1)
    climb(3, 2)
    climb(3, 3)
    up_on((4, 3), (3, 1))
    climb(2, 0)
    climb(2, 1)
    at_place(2)
    up_on((3, 3))
    climb(2, 2)
    climb(2, 3)
    climb(1, 0)
    up_on((2, 1))
    at_place(3)
    climb(1, 2)
    climb(1, 3)
    climb(1, 1)
    climb(0, 0)
    climb(0, 1)
    image_result(0)
    at_place(4)
    over_all.wait_recv()
    both_out[1] = back_norm(txt_ref[...], inv_txt, text_sum[0:ROWS] + row_in[...].astype(F32))
    climb(0, 2)
    climb(0, 3)
    image_result(1)

    def all_left(ref, leaves):
        remote(ref, ref, twin, leaves, 0).wait_send()

    all_left(imgs, TWIN)
    all_left(txts, TEXT)
    all_left(imgs.at[0:3], PART)
    all_left(relay_down, DOWN)
    all_left(chain_out, UP)

    @pl.when(first_z)
    def _():
        all_left(relay_down, DOWN + 1)

    @pl.when(last_z)
    def _():
        all_left(relay_up, UP + 1)


N_ARRIVALS = 2 * 16 + 6 + 7 + 3 + (16 + 4) + 7


def per_device(loops, images, texts, factor, shift):
    smem = pl.BlockSpec(memory_space=pltpu.SMEM)
    hbm = pl.BlockSpec(memory_space=pltpu.HBM)
    vmem = pl.BlockSpec(memory_space=pltpu.VMEM)
    out = jax.ShapeDtypeStruct((2, ROWS, WIDE), F32)
    both = pl.pallas_call(
        functools.partial(kernel, loops),
        out_shape=out,
        in_specs=[smem, smem, hbm, hbm],
        out_specs=vmem,
        scratch_shapes=[
            pltpu.VMEM((ROWS, WIDE), BF16),
            pltpu.VMEM((ROWS, WIDE), BF16),
            pltpu.VMEM((HOPS + 1, 2, ROWS, WIDE), BF16),
            pltpu.VMEM((2, XS, ROWS, WIDE), BF16),
            pltpu.VMEM((HOPS + 1, 2, ROWS, WORDS), BF16),
            pltpu.VMEM((HOPS + 1, ROWS, WIDE), F32),
            pltpu.VMEM((WORDS, WIDE), F32),
            pltpu.VMEM((HOPS + 1, ROWS, WIDE), BF16),
            pltpu.VMEM((HOPS + 1, ROWS, WIDE), BF16),
            pltpu.VMEM((HOPS, ROWS, WIDE), BF16),
            pltpu.VMEM((HOPS, ROWS, WIDE), BF16),
            pltpu.VMEM((2, XS, ROWS, WIDE), BF16),
            pltpu.VMEM((2, HALF, WIDE), BF16),
            pltpu.VMEM((2, HALF, WIDE), BF16),
            pltpu.VMEM((2, 2, ROWS, WIDE), BF16),
            pltpu.VMEM((ROWS, WIDE), BF16),
            pltpu.VMEM((ROWS, WIDE), BF16),
            pltpu.SemaphoreType.DMA((2,)),
            pltpu.SemaphoreType.REGULAR,
            pltpu.VMEM((HOPS, ROWS, WIDE), BF16),
            pltpu.VMEM((len(ROUND), SLICE, WIDE), BF16),
            pltpu.SemaphoreType.DMA((N_LEAVES,)),
            pltpu.SemaphoreType.DMA((N_ARRIVALS,)),
        ],
        compiler_params=pltpu.CompilerParams(
            collective_id=0, has_side_effects=True, vmem_limit_bytes=48 * 2**20
        ),
        name="siglip",
    )(
        factor,
        shift,
        pltpu.with_memory_space_constraint(images, pltpu.HBM),
        pltpu.with_memory_space_constraint(texts, pltpu.HBM),
    )
    return both[0], both[1]


def solution(mesh):
    loops = mesh.shape["loop"]
    spec = P(("grp", "loop"), None)

    def step(images, texts, factor, shift):
        return per_device(loops, images, texts, factor, shift)

    return jax.shard_map(
        step, mesh=mesh, in_specs=(spec, spec, P(), P()), out_specs=(spec, spec), check_vma=False
    )
```

```python
import functools

import jax
import jax.numpy as jnp
from jax import lax
from jax.experimental import pallas as pl
from jax.experimental.pallas import tpu as pltpu
from jax.sharding import PartitionSpec as P

HOPS = 4
ROWS = 64
HALF = 32
SLICE = 16
SLICES = ROWS // SLICE
WIDE = 1536
XS = 4
ZS = 16
MINE = XS * ROWS
WORDS = 2 * MINE
DOWN, UP, TWIN, TEXT, PART = 0, 2, 4, 5, 6
N_LEAVES = 7
ROUND = ((4, 3), (3, 1), (3, 3), (2, 1))
MESH = pl.DeviceIdType.MESH
F32 = jnp.float32
BF16 = jnp.bfloat16
BOTH_LAST = (((1,), (1,)), ((), ()))
BOTH_FIRST = (((0,), (0,)), ((), ()))


def half(c):
    return pl.ds(c * HALF, HALF)


def sliver(u):
    return pl.ds(u * SLICE, SLICE)


def inverse_norm(ref):
    wide = ref[...].astype(F32)
    return lax.rsqrt(jnp.sum(wide * wide, axis=-1, keepdims=True) + 1e-06)


def back_norm(raw, inverse, grad):
    unit = raw.astype(F32) * inverse
    return (grad - unit * jnp.sum(unit * grad, axis=-1, keepdims=True)) * inverse


def kernel(
    loops,
    factor_ref,
    shift_ref,
    img_hbm,
    txt_hbm,
    both_out,
    img_ref,
    txt_ref,
    imgs,
    txts,
    coefs,
    grads,
    text_sum,
    other_out,
    other_in,
    chain_out,
    chain_in,
    part_out,
    first_a,
    first_b,
    second,
    row_out,
    row_in,
    load_sem,
    go_sem,
    relay_down,
    relay_up,
    send_sem,
    recv_sem,
):
    g = lax.axis_index("grp")
    q = lax.axis_index("loop")
    x = g // 4
    y = (g // 2) % 2
    core = g % 2
    z = q % ZS

    def member(xx, yy, cc):
        return {"grp": xx * 4 + yy * 2 + cc, "loop": q}

    twin = member(x, y, 1 - core)
    across = member(x, 1 - y, core)
    right = member((x + 1) % XS, y, core)
    left = member((x + XS - 1) % XS, y, core)
    below = {"grp": g, "loop": (q + loops - 1) % loops}
    above = {"grp": g, "loop": (q + 1) % loops}
    first_z = z == 0
    last_z = z == ZS - 1
    far_below = {"grp": across["grp"], "loop": below["loop"]}
    far_above = {"grp": across["grp"], "loop": above["loop"]}

    loads = [
        pltpu.make_async_copy(txt_hbm, txt_ref, load_sem.at[0]),
        pltpu.make_async_copy(img_hbm, img_ref, load_sem.at[1]),
    ]
    for load in loads:
        load.start()

    barrier = pltpu.get_barrier_semaphore()
    for peer in (twin, across, right, left):
        pl.semaphore_signal(barrier, inc=1, device_id=peer, device_id_type=MESH)

    @pl.when(first_z)
    def _():
        pl.semaphore_signal(barrier, inc=1, device_id=far_below, device_id_type=MESH)

    pl.semaphore_signal(barrier, inc=1, device_id=below, device_id_type=MESH)

    @pl.when(jnp.logical_not(last_z))
    def _():
        pl.semaphore_signal(barrier, inc=1, device_id=above, device_id_type=MESH)

    used = [0]

    def arrival():
        used[0] += 1
        return used[0] - 1

    def remote(src, dst, device, leaves, lands):
        return pltpu.make_async_remote_copy(
            src_ref=src,
            dst_ref=dst,
            send_sem=send_sem.at[leaves],
            recv_sem=recv_sem.at[lands],
            device_id=device,
            device_id_type=MESH,
        )

    def link(src, dst, device, leaves, lands=None):
        return remote(src, dst, device, leaves, arrival() if lands is None else lands)

    class LoopLink:
        def __init__(self, src, dst, device, leaves, at_edge, relay, onto):
            self.at_edge, self.relay = at_edge, relay
            lands = arrival()
            self.plain = remote(src, dst, device, leaves, lands)
            if relay is not None:
                self.aside = remote(src, relay, across, leaves, arrival())
                self.onward = remote(relay, dst, onto, leaves + 1, lands)

        def start(self):
            if self.relay is None:
                self.plain.start()
            else:
                pl.when(jnp.logical_not(self.at_edge))(self.plain.start)
                pl.when(self.at_edge)(self.aside.start)

        def send_on(self):
            self.aside.wait_recv()
            self.onward.start()

        def wait_recv(self):
            self.plain.wait_recv()

    down = {
        (h, u): LoopLink(
            imgs.at[h - 1, 0, sliver(u)],
            imgs.at[h, 0, sliver(u)],
            below,
            DOWN,
            first_z,
            relay_down.at[h - 1, sliver(u)],
            far_below,
        )
        for h in range(1, HOPS + 1)
        for u in range(SLICES)
    }
    to_twin = [link(imgs.at[0, 0], imgs.at[0, 1], twin, TWIN)]
    to_twin_half = {}
    for h in range(1, HOPS + 1):
        lands = arrival()
        for c in range(2):
            alone = lands if h < HOPS or c == 0 else arrival()
            to_twin_half[h, c] = link(
                imgs.at[h, 0, half(c)], imgs.at[h, 1, half(c)], twin, TWIN, alone
            )
        if h < HOPS:
            to_twin.append(link(imgs.at[h, 0], imgs.at[h, 1], twin, TWIN, lands))
    text_y = [
        link(txts.at[0, 0, half(c)], txts.at[1, 0, half(c)], across, TEXT) for c in range(2)
    ]
    text_last = arrival()
    text_right = {
        (r, c): link(
            txts.at[r, 0, half(c)],
            txts.at[r, 3, half(c)],
            right,
            TEXT,
            arrival() if c == 0 else text_last,
        )
        for r in range(2)
        for c in range(2)
    }
    text_left = {
        (r, c): link(
            txts.at[r, 0, half(c)],
            txts.at[r, 1, half(c)],
            left,
            TEXT,
            arrival() if c == 1 else text_last,
        )
        for r in range(2)
        for c in range(2)
    }
    text_far_a = [
        link(txts.at[r, 3, half(0)], txts.at[r, 2, half(0)], right, TEXT, text_last)
        for r in range(2)
    ]
    text_far_b = [
        link(txts.at[r, 1, half(1)], txts.at[r, 2, half(1)], left, TEXT, text_last)
        for r in range(2)
    ]
    text_rest = link(txts.at[0], txts.at[0], right, TEXT, text_last)
    term_early = link(other_out.at[0:HOPS], other_in.at[0:HOPS], twin, TWIN)
    term_last = [
        link(other_out.at[HOPS, half(c)], other_in.at[HOPS, half(c)], twin, TWIN) for c in range(2)
    ]
    up = {
        (h, u): LoopLink(
            chain_out.at[h - 1, sliver(u)],
            chain_in.at[h - 1, sliver(u)],
            above,
            UP,
            last_z,
            relay_up.at[ROUND.index((h, u))] if (h, u) in ROUND else None,
            far_above,
        )
        for h in range(1, HOPS + 1)
        for u in range(SLICES)
    }
    far_a = [link(part_out.at[r, 2, half(0)], first_a.at[r], right, PART) for r in range(2)]
    far_b = [link(part_out.at[r, 2, half(1)], first_b.at[r], left, PART) for r in range(2)]
    row_lands = [arrival() for _ in range(2)]
    near_right = {
        (r, c): link(
            part_out.at[r, 1, half(c)], second.at[r, 0, half(c)], right, PART, row_lands[r]
        )
        for r in range(2)
        for c in range(2)
    }
    near_left = {
        (r, c): link(
            part_out.at[r, 3, half(c)], second.at[r, 1, half(c)], left, PART, row_lands[r]
        )
        for r in range(2)
        for c in range(2)
    }
    near_rows = [link(second.at[r], second.at[r], right, PART, row_lands[r]) for r in range(2)]
    over_lands = arrival()
    over = [link(row_out.at[half(c)], row_in.at[half(c)], across, TEXT, over_lands) for c in range(2)]
    over_all = link(row_out, row_in, across, TEXT, over_lands)
    assert used[0] == N_ARRIVALS, used[0]

    factor = factor_ref[0]
    shift = shift_ref[0]

    @pl.when(last_z)
    def _():
        pl.semaphore_wait(barrier, 7)
        pl.semaphore_signal(go_sem, inc=1, device_id=far_above, device_id_type=MESH)

    loads[0].wait()
    inv_txt = inverse_norm(txt_ref)
    txts[0, 0] = (txt_ref[...].astype(F32) * inv_txt).astype(BF16)
    loads[1].wait()
    inv_img = inverse_norm(img_ref)
    imgs[0, 0] = (img_ref[...].astype(F32) * inv_img).astype(BF16)

    @pl.when(first_z)
    def _():
        pl.semaphore_wait(barrier, 5)

    @pl.when(jnp.logical_not(jnp.logical_or(first_z, last_z)))
    def _():
        pl.semaphore_wait(barrier, 6)

    for c in range(2):
        text_y[c].start()
        for u in (2 * c, 2 * c + 1):
            pl.when(jnp.logical_not(first_z))(down[1, u].start)
        text_right[0, c].start()
        text_left[0, c].start()
    for u in range(SLICES):
        pl.when(first_z)(down[1, u].start)
    to_twin[0].start()

    def pass_on(h, *slivers):
        for u in slivers:
            down[h, u].wait_recv()
            if h == 1:
                pl.when(jnp.logical_not(first_z))(down[2, u].start)
            elif h < HOPS:
                down[h + 1, u].start()
            if u % 2:
                to_twin_half[h, u // 2].start()

    def send_on(links, at_edge, *keys):
        @pl.when(at_edge)
        def _():
            for key in keys:
                links[key].send_on()

    down_on = functools.partial(send_on, down, first_z)
    up_on = functools.partial(send_on, up, last_z)

    def from_twin(h):
        to_twin[h].wait_recv()

    def spread_row(c):
        text_y[c].wait_recv()
        text_right[1, c].start()
        text_left[1, c].start()

    def coef_of(s):
        return jax.nn.sigmoid(s * factor + shift) * factor

    def scores(pictures):
        return lax.dot_general(
            pictures, txts[...].reshape(WORDS, WIDE), BOTH_LAST, preferred_element_type=F32
        )

    def coef_hops(lo, hi):
        s = scores(imgs[lo:hi].reshape((hi - lo) * 2 * ROWS, WIDE))
        coefs[lo:hi] = coef_of(s).astype(BF16).reshape(hi - lo, 2, ROWS, WORDS)
        if lo == 0:
            own = s[0:ROWS, 0:128] * factor + shift
            rows = lax.broadcasted_iota(jnp.int32, own.shape, 0)
            cols = lax.broadcasted_iota(jnp.int32, own.shape, 1)
            sign = jnp.where(rows == cols, 1.0, -1.0).astype(F32)
            value = -sign * jax.nn.sigmoid(-sign * own) * factor
            coefs[0, 0, :, 0:128] = value.astype(BF16)

    def coef_half(h, c):
        s = scores(imgs[h, :, c * HALF : (c + 1) * HALF].reshape(2 * HALF, WIDE))
        coefs[h, :, c * HALF : (c + 1) * HALF] = coef_of(s).astype(BF16).reshape(2, HALF, WORDS)

    def terms_hops(lo, hi):
        out = jnp.dot(
            coefs[lo:hi].reshape((hi - lo) * 2 * ROWS, WORDS),
            txts[...].reshape(WORDS, WIDE),
            preferred_element_type=F32,
        ).reshape(hi - lo, 2, ROWS, WIDE)
        grads[lo:hi] = out[:, 0]
        other_out[lo:hi] = out[:, 1].astype(BF16)
        term_early.start()

    def terms_half(h, c):
        out = jnp.dot(
            coefs[h, :, c * HALF : (c + 1) * HALF].reshape(2 * HALF, WORDS),
            txts[...].reshape(WORDS, WIDE),
            preferred_element_type=F32,
        ).reshape(2, HALF, WIDE)
        grads[h, half(c)] = out[0]
        other_out[h, half(c)] = out[1].astype(BF16)
        term_last[c].start()

    def climb(h, u):
        if h == HOPS and u % 2 == 0:
            term_last[u // 2].wait_recv()
        if h == HOPS - 1 and u == 0:
            term_early.wait_recv()
        total = grads[h, sliver(u)] + other_in[h, sliver(u)].astype(F32)
        if h < HOPS:
            up[h + 1, u].wait_recv()
            total = total + chain_in[h, sliver(u)].astype(F32)
        if h > 0:
            chain_out[h - 1, sliver(u)] = total.astype(BF16)
            up[h, u].start()
        else:
            grads[0, sliver(u)] = total

    def far_text(side):
        (text_right[1, 0] if side == 0 else text_left[1, 1]).wait_recv()
        (text_far_a[1] if side == 0 else text_far_b[1]).start()

    not_last = jnp.logical_not(last_z)
    pl.when(not_last)(functools.partial(pass_on, 1, 0))
    spread_row(0)
    pl.when(last_z)(functools.partial(pass_on, 1, 0))
    pass_on(1, 1, 2)
    spread_row(1)
    text_right[0, 0].wait_recv()
    text_far_a[0].start()
    pass_on(1, 3)
    text_left[0, 1].wait_recv()
    text_far_b[0].start()

    @pl.when(first_z)
    def _():
        down[2, 0].start()
        down[2, 1].start()
        pl.semaphore_wait(go_sem, 1)

    down_on((1, 0), (1, 1), (1, 2), (1, 3))
    for u in (2, 3):
        pl.when(first_z)(down[2, u].start)
    pl.when(last_z)(functools.partial(far_text, 0))
    pass_on(2, 0, 1)
    pl.when(not_last)(functools.partial(far_text, 0))
    pl.when(last_z)(functools.partial(far_text, 1))
    pass_on(2, 2, 3)
    pl.when(not_last)(functools.partial(far_text, 1))
    down_on((2, 0), (2, 1))
    pass_on(3, 0)
    down_on((2, 2), (2, 3))
    pass_on(3, 1)
    down_on((3, 0))
    pass_on(3, 2)
    down_on((3, 1))
    pass_on(3, 3)
    down_on((3, 2))
    text_rest.wait_recv()
    down_on((3, 3))
    for h in range(2):
        from_twin(h)
    coef_hops(0, 2)
    pass_on(4, 0, 1)
    down_on((4, 0), (4, 1))
    for h in range(2, 4):
        from_twin(h)
    coef_hops(2, 4)
    down_on((4, 2), (4, 3))
    to_twin_half[4, 0].wait_recv()
    coef_half(4, 0)
    terms_half(4, 0)
    pass_on(4, 2, 3)
    terms_hops(0, 4)
    climb(4, 0)
    climb(4, 1)

    def text_row(r):
        at = r * MINE
        total = lax.dot_general(
            coefs[:, :, :, at : at + MINE].reshape((HOPS + 1) * 2 * ROWS, MINE),
            imgs[...].reshape((HOPS + 1) * 2 * ROWS, WIDE),
            BOTH_FIRST,
            preferred_element_type=F32,
        )
        text_sum[at : at + MINE] = total
        part_out[r] = total.astype(BF16).reshape(XS, ROWS, WIDE)

    def join(r):
        far_a[r].wait_recv()
        at = (r * XS + 1) * ROWS
        part_out[r, 1, half(0)] = (text_sum[at : at + HALF] + first_a[r].astype(F32)).astype(BF16)
        near_right[r, 0].start()
        far_b[r].wait_recv()
        at = (r * XS + 3) * ROWS + HALF
        part_out[r, 3, half(1)] = (text_sum[at : at + HALF] + first_b[r].astype(F32)).astype(BF16)
        near_left[r, 1].start()

    def row_total(r):
        near_rows[r].wait_recv()
        at = r * MINE
        return (
            text_sum[at : at + ROWS]
            + second[r, 0].astype(F32)
            + second[r, 1].astype(F32)
        )

    def join_rows():
        join(1)
        near_right[0, 1].start()
        near_left[0, 0].start()

    def image_result(c):
        rows = slice(c * HALF, (c + 1) * HALF)
        both_out[0, rows] = back_norm(img_ref[rows], inv_img[rows], grads[0, rows])

    to_twin_half[4, 1].wait_recv()
    coef_half(4, 1)
    terms_half(4, 1)
    text_row(1)
    far_a[1].start()
    far_b[1].start()
    near_right[1, 1].start()
    near_left[1, 0].start()
    climb(4, 2)
    climb(4, 3)
    text_row(0)
    far_a[0].start()
    far_b[0].start()

    def sum_row():
        row_out[...] = row_total(1).astype(BF16)
        for c in range(2):
            over[c].start()

    def own_row():
        text_sum[0:ROWS] = row_total(0)

    steps = (join_rows, functools.partial(join, 0), sum_row, own_row)

    usual = (1, 2, 3, 4)
    high = range(ZS - HOPS, ZS)
    moved = (
        {0: 0} | dict.fromkeys(high, 2),
        {0: 0, 1: 1} | dict.fromkeys(high, 3),
        {0: 1, 1: 2, 2: 2} | dict.fromkeys(high, 4),
        {0: 2, 1: 3, 2: 3, 3: 3},
    )

    def at_place(place):
        for step, common, others in zip(steps, usual, moved):
            if place == common:
                here = functools.reduce(jnp.logical_and, [z != at for at in others if others[at] != place])
                pl.when(here)(step)
            else:
                chosen = [z == at for at in others if others[at] == place]
                if chosen:
                    pl.when(functools.reduce(jnp.logical_or, chosen))(step)

    at_place(0)
    climb(3, 0)
    climb(3, 1)
    at_place(1)
    climb(3, 2)
    climb(3, 3)
    up_on((4, 3), (3, 1))
    climb(2, 0)
    climb(2, 1)
    at_place(2)
    up_on((3, 3))
    climb(2, 2)
    climb(2, 3)
    climb(1, 0)
    up_on((2, 1))
    at_place(3)
    climb(1, 2)
    climb(1, 3)
    climb(1, 1)
    climb(0, 0)
    climb(0, 2)
    climb(0, 3)
    image_result(1)
    at_place(4)
    over_all.wait_recv()
    both_out[1] = back_norm(txt_ref[...], inv_txt, text_sum[0:ROWS] + row_in[...].astype(F32))
    climb(0, 1)
    image_result(0)

    def all_left(ref, leaves):
        remote(ref, ref, twin, leaves, 0).wait_send()

    all_left(imgs, TWIN)
    all_left(txts, TEXT)
    all_left(imgs.at[0:3], PART)
    all_left(relay_down, DOWN)
    all_left(chain_out, UP)

    @pl.when(first_z)
    def _():
        all_left(relay_down, DOWN + 1)

    @pl.when(last_z)
    def _():
        all_left(relay_up, UP + 1)


N_ARRIVALS = 2 * 16 + 6 + 7 + 3 + (16 + 4) + 7


def per_device(loops, images, texts, factor, shift):
    smem = pl.BlockSpec(memory_space=pltpu.SMEM)
    hbm = pl.BlockSpec(memory_space=pltpu.HBM)
    vmem = pl.BlockSpec(memory_space=pltpu.VMEM)
    out = jax.ShapeDtypeStruct((2, ROWS, WIDE), F32)
    both = pl.pallas_call(
        functools.partial(kernel, loops),
        out_shape=out,
        in_specs=[smem, smem, hbm, hbm],
        out_specs=vmem,
        scratch_shapes=[
            pltpu.VMEM((ROWS, WIDE), BF16),
            pltpu.VMEM((ROWS, WIDE), BF16),
            pltpu.VMEM((HOPS + 1, 2, ROWS, WIDE), BF16),
            pltpu.VMEM((2, XS, ROWS, WIDE), BF16),
            pltpu.VMEM((HOPS + 1, 2, ROWS, WORDS), BF16),
            pltpu.VMEM((HOPS + 1, ROWS, WIDE), F32),
            pltpu.VMEM((WORDS, WIDE), F32),
            pltpu.VMEM((HOPS + 1, ROWS, WIDE), BF16),
            pltpu.VMEM((HOPS + 1, ROWS, WIDE), BF16),
            pltpu.VMEM((HOPS, ROWS, WIDE), BF16),
            pltpu.VMEM((HOPS, ROWS, WIDE), BF16),
            pltpu.VMEM((2, XS, ROWS, WIDE), BF16),
            pltpu.VMEM((2, HALF, WIDE), BF16),
            pltpu.VMEM((2, HALF, WIDE), BF16),
            pltpu.VMEM((2, 2, ROWS, WIDE), BF16),
            pltpu.VMEM((ROWS, WIDE), BF16),
            pltpu.VMEM((ROWS, WIDE), BF16),
            pltpu.SemaphoreType.DMA((2,)),
            pltpu.SemaphoreType.REGULAR,
            pltpu.VMEM((HOPS, ROWS, WIDE), BF16),
            pltpu.VMEM((len(ROUND), SLICE, WIDE), BF16),
            pltpu.SemaphoreType.DMA((N_LEAVES,)),
            pltpu.SemaphoreType.DMA((N_ARRIVALS,)),
        ],
        compiler_params=pltpu.CompilerParams(
            collective_id=0, has_side_effects=True, vmem_limit_bytes=48 * 2**20
        ),
        name="siglip",
    )(
        factor,
        shift,
        pltpu.with_memory_space_constraint(images, pltpu.HBM),
        pltpu.with_memory_space_constraint(texts, pltpu.HBM),
    )
    return both[0], both[1]


def solution(mesh):
    loops = mesh.shape["loop"]
    spec = P(("grp", "loop"), None)

    def step(images, texts, factor, shift):
        return per_device(loops, images, texts, factor, shift)

    return jax.shard_map(
        step, mesh=mesh, in_specs=(spec, spec, P(), P()), out_specs=(spec, spec), check_vma=False
    )
```

```python
import functools

import jax
import jax.numpy as jnp
from jax import lax
from jax.experimental import pallas as pl
from jax.experimental.pallas import tpu as pltpu
from jax.sharding import PartitionSpec as P

HOPS = 4
ROWS = 64
HALF = 32
SLICE = 16
SLICES = ROWS // SLICE
WIDE = 1536
XS = 4
ZS = 16
MINE = XS * ROWS
WORDS = 2 * MINE
DOWN, UP, TWIN, TEXT, PART = 0, 2, 4, 5, 6
N_LEAVES = 7
ROUND = ((4, 3), (3, 1), (3, 3), (2, 1))
MESH = pl.DeviceIdType.MESH
F32 = jnp.float32
BF16 = jnp.bfloat16
BOTH_LAST = (((1,), (1,)), ((), ()))
BOTH_FIRST = (((0,), (0,)), ((), ()))


def half(c):
    return pl.ds(c * HALF, HALF)


def sliver(u):
    return pl.ds(u * SLICE, SLICE)


def inverse_norm(ref):
    wide = ref[...].astype(F32)
    return lax.rsqrt(jnp.sum(wide * wide, axis=-1, keepdims=True) + 1e-06)


def back_norm(raw, inverse, grad):
    unit = raw.astype(F32) * inverse
    return (grad - unit * jnp.sum(unit * grad, axis=-1, keepdims=True)) * inverse


def kernel(
    loops,
    factor_ref,
    shift_ref,
    img_hbm,
    txt_hbm,
    both_out,
    img_ref,
    txt_ref,
    imgs,
    txts,
    coefs,
    grads,
    text_sum,
    other_out,
    other_in,
    chain_out,
    chain_in,
    part_out,
    first_a,
    first_b,
    second,
    row_out,
    row_in,
    load_sem,
    go_sem,
    relay_down,
    relay_up,
    send_sem,
    recv_sem,
):
    g = lax.axis_index("grp")
    q = lax.axis_index("loop")
    x = g // 4
    y = (g // 2) % 2
    core = g % 2
    z = q % ZS

    def member(xx, yy, cc):
        return {"grp": xx * 4 + yy * 2 + cc, "loop": q}

    twin = member(x, y, 1 - core)
    across = member(x, 1 - y, core)
    right = member((x + 1) % XS, y, core)
    left = member((x + XS - 1) % XS, y, core)
    below = {"grp": g, "loop": (q + loops - 1) % loops}
    above = {"grp": g, "loop": (q + 1) % loops}
    first_z = z == 0
    last_z = z == ZS - 1
    far_below = {"grp": across["grp"], "loop": below["loop"]}
    far_above = {"grp": across["grp"], "loop": above["loop"]}

    loads = [
        pltpu.make_async_copy(txt_hbm, txt_ref, load_sem.at[0]),
        pltpu.make_async_copy(img_hbm, img_ref, load_sem.at[1]),
    ]
    for load in loads:
        load.start()

    barrier = pltpu.get_barrier_semaphore()
    for peer in (twin, across, right, left):
        pl.semaphore_signal(barrier, inc=1, device_id=peer, device_id_type=MESH)

    @pl.when(first_z)
    def _():
        pl.semaphore_signal(barrier, inc=1, device_id=far_below, device_id_type=MESH)

    pl.semaphore_signal(barrier, inc=1, device_id=below, device_id_type=MESH)

    @pl.when(jnp.logical_not(last_z))
    def _():
        pl.semaphore_signal(barrier, inc=1, device_id=above, device_id_type=MESH)

    used = [0]

    def arrival():
        used[0] += 1
        return used[0] - 1

    def remote(src, dst, device, leaves, lands):
        return pltpu.make_async_remote_copy(
            src_ref=src,
            dst_ref=dst,
            send_sem=send_sem.at[leaves],
            recv_sem=recv_sem.at[lands],
            device_id=device,
            device_id_type=MESH,
        )

    def link(src, dst, device, leaves, lands=None):
        return remote(src, dst, device, leaves, arrival() if lands is None else lands)

    class LoopLink:
        def __init__(self, src, dst, device, leaves, at_edge, relay, onto):
            self.at_edge, self.relay = at_edge, relay
            lands = arrival()
            self.plain = remote(src, dst, device, leaves, lands)
            if relay is not None:
                self.aside = remote(src, relay, across, leaves, arrival())
                self.onward = remote(relay, dst, onto, leaves + 1, lands)

        def start(self):
            if self.relay is None:
                self.plain.start()
            else:
                pl.when(jnp.logical_not(self.at_edge))(self.plain.start)
                pl.when(self.at_edge)(self.aside.start)

        def send_on(self):
            self.aside.wait_recv()
            self.onward.start()

        def wait_recv(self):
            self.plain.wait_recv()

    down = {
        (h, u): LoopLink(
            imgs.at[h - 1, 0, sliver(u)],
            imgs.at[h, 0, sliver(u)],
            below,
            DOWN,
            first_z,
            relay_down.at[h - 1, sliver(u)],
            far_below,
        )
        for h in range(1, HOPS + 1)
        for u in range(SLICES)
    }
    to_twin = [link(imgs.at[0, 0], imgs.at[0, 1], twin, TWIN)]
    to_twin_half = {}
    for h in range(1, HOPS + 1):
        lands = arrival()
        for c in range(2):
            alone = lands if h < HOPS or c == 0 else arrival()
            to_twin_half[h, c] = link(
                imgs.at[h, 0, half(c)], imgs.at[h, 1, half(c)], twin, TWIN, alone
            )
        if h < HOPS:
            to_twin.append(link(imgs.at[h, 0], imgs.at[h, 1], twin, TWIN, lands))
    text_y = [
        link(txts.at[0, 0, half(c)], txts.at[1, 0, half(c)], across, TEXT) for c in range(2)
    ]
    text_last = arrival()
    text_right = {
        (r, c): link(
            txts.at[r, 0, half(c)],
            txts.at[r, 3, half(c)],
            right,
            TEXT,
            arrival() if c == 0 else text_last,
        )
        for r in range(2)
        for c in range(2)
    }
    text_left = {
        (r, c): link(
            txts.at[r, 0, half(c)],
            txts.at[r, 1, half(c)],
            left,
            TEXT,
            arrival() if c == 1 else text_last,
        )
        for r in range(2)
        for c in range(2)
    }
    text_far_a = [
        link(txts.at[r, 3, half(0)], txts.at[r, 2, half(0)], right, TEXT, text_last)
        for r in range(2)
    ]
    text_far_b = [
        link(txts.at[r, 1, half(1)], txts.at[r, 2, half(1)], left, TEXT, text_last)
        for r in range(2)
    ]
    text_rest = link(txts.at[0], txts.at[0], right, TEXT, text_last)
    term_early = link(other_out.at[0:HOPS], other_in.at[0:HOPS], twin, TWIN)
    term_last = [
        link(other_out.at[HOPS, half(c)], other_in.at[HOPS, half(c)], twin, TWIN) for c in range(2)
    ]
    up = {
        (h, u): LoopLink(
            chain_out.at[h - 1, sliver(u)],
            chain_in.at[h - 1, sliver(u)],
            above,
            UP,
            last_z,
            relay_up.at[ROUND.index((h, u))] if (h, u) in ROUND else None,
            far_above,
        )
        for h in range(1, HOPS + 1)
        for u in range(SLICES)
    }
    far_a = [link(part_out.at[r, 2, half(0)], first_a.at[r], right, PART) for r in range(2)]
    far_b = [link(part_out.at[r, 2, half(1)], first_b.at[r], left, PART) for r in range(2)]
    row_lands = [arrival() for _ in range(2)]
    near_right = {
        (r, c): link(
            part_out.at[r, 1, half(c)], second.at[r, 0, half(c)], right, PART, row_lands[r]
        )
        for r in range(2)
        for c in range(2)
    }
    near_left = {
        (r, c): link(
            part_out.at[r, 3, half(c)], second.at[r, 1, half(c)], left, PART, row_lands[r]
        )
        for r in range(2)
        for c in range(2)
    }
    near_rows = [link(second.at[r], second.at[r], right, PART, row_lands[r]) for r in range(2)]
    over_lands = arrival()
    over = [link(row_out.at[half(c)], row_in.at[half(c)], across, TEXT, over_lands) for c in range(2)]
    over_all = link(row_out, row_in, across, TEXT, over_lands)
    assert used[0] == N_ARRIVALS, used[0]

    factor = factor_ref[0]
    shift = shift_ref[0]

    @pl.when(last_z)
    def _():
        pl.semaphore_wait(barrier, 7)
        pl.semaphore_signal(go_sem, inc=1, device_id=far_above, device_id_type=MESH)

    loads[0].wait()
    inv_txt = inverse_norm(txt_ref)
    txts[0, 0] = (txt_ref[...].astype(F32) * inv_txt).astype(BF16)
    loads[1].wait()
    inv_img = inverse_norm(img_ref)
    imgs[0, 0] = (img_ref[...].astype(F32) * inv_img).astype(BF16)

    @pl.when(first_z)
    def _():
        pl.semaphore_wait(barrier, 5)

    @pl.when(jnp.logical_not(jnp.logical_or(first_z, last_z)))
    def _():
        pl.semaphore_wait(barrier, 6)

    for c in range(2):
        text_y[c].start()
        for u in (2 * c, 2 * c + 1):
            pl.when(jnp.logical_not(first_z))(down[1, u].start)
        text_right[0, c].start()
        text_left[0, c].start()
    for u in range(SLICES):
        pl.when(first_z)(down[1, u].start)
    to_twin[0].start()

    def pass_on(h, *slivers):
        for u in slivers:
            down[h, u].wait_recv()
            if h == 1:
                pl.when(jnp.logical_not(first_z))(down[2, u].start)
            elif h < HOPS:
                down[h + 1, u].start()
            if u % 2:
                to_twin_half[h, u // 2].start()

    def send_on(links, at_edge, *keys):
        @pl.when(at_edge)
        def _():
            for key in keys:
                links[key].send_on()

    down_on = functools.partial(send_on, down, first_z)
    up_on = functools.partial(send_on, up, last_z)

    def from_twin(h):
        to_twin[h].wait_recv()

    def spread_row(c):
        text_y[c].wait_recv()
        text_right[1, c].start()
        text_left[1, c].start()

    def coef_of(s):
        return jax.nn.sigmoid(s * factor + shift) * factor

    def scores(pictures):
        return lax.dot_general(
            pictures, txts[...].reshape(WORDS, WIDE), BOTH_LAST, preferred_element_type=F32
        )

    def coef_hops(lo, hi):
        s = scores(imgs[lo:hi].reshape((hi - lo) * 2 * ROWS, WIDE))
        coefs[lo:hi] = coef_of(s).astype(BF16).reshape(hi - lo, 2, ROWS, WORDS)
        if lo == 0:
            own = s[0:ROWS, 0:128] * factor + shift
            rows = lax.broadcasted_iota(jnp.int32, own.shape, 0)
            cols = lax.broadcasted_iota(jnp.int32, own.shape, 1)
            sign = jnp.where(rows == cols, 1.0, -1.0).astype(F32)
            value = -sign * jax.nn.sigmoid(-sign * own) * factor
            coefs[0, 0, :, 0:128] = value.astype(BF16)

    def coef_half(h, c):
        s = scores(imgs[h, :, c * HALF : (c + 1) * HALF].reshape(2 * HALF, WIDE))
        coefs[h, :, c * HALF : (c + 1) * HALF] = coef_of(s).astype(BF16).reshape(2, HALF, WORDS)

    def terms_hops(lo, hi):
        out = jnp.dot(
            coefs[lo:hi].reshape((hi - lo) * 2 * ROWS, WORDS),
            txts[...].reshape(WORDS, WIDE),
            preferred_element_type=F32,
        ).reshape(hi - lo, 2, ROWS, WIDE)
        grads[lo:hi] = out[:, 0]
        other_out[lo:hi] = out[:, 1].astype(BF16)
        term_early.start()

    def terms_half(h, c):
        out = jnp.dot(
            coefs[h, :, c * HALF : (c + 1) * HALF].reshape(2 * HALF, WORDS),
            txts[...].reshape(WORDS, WIDE),
            preferred_element_type=F32,
        ).reshape(2, HALF, WIDE)
        grads[h, half(c)] = out[0]
        other_out[h, half(c)] = out[1].astype(BF16)
        term_last[c].start()

    def climb(h, u):
        if h == HOPS and u % 2 == 0:
            term_last[u // 2].wait_recv()
        if h == HOPS - 1 and u == 0:
            term_early.wait_recv()
        total = grads[h, sliver(u)] + other_in[h, sliver(u)].astype(F32)
        if h < HOPS:
            up[h + 1, u].wait_recv()
            total = total + chain_in[h, sliver(u)].astype(F32)
        if h > 0:
            chain_out[h - 1, sliver(u)] = total.astype(BF16)
            up[h, u].start()
        else:
            grads[0, sliver(u)] = total

    def far_text(side):
        (text_right[1, 0] if side == 0 else text_left[1, 1]).wait_recv()
        (text_far_a[1] if side == 0 else text_far_b[1]).start()

    not_last = jnp.logical_not(last_z)
    pl.when(not_last)(functools.partial(pass_on, 1, 0))
    spread_row(0)
    pl.when(last_z)(functools.partial(pass_on, 1, 0))
    pass_on(1, 1, 2)
    spread_row(1)
    text_right[0, 0].wait_recv()
    text_far_a[0].start()
    pass_on(1, 3)
    text_left[0, 1].wait_recv()
    text_far_b[0].start()

    @pl.when(first_z)
    def _():
        down[2, 0].start()
        down[2, 1].start()
        pl.semaphore_wait(go_sem, 1)

    down_on((1, 0), (1, 1), (1, 2), (1, 3))
    for u in (2, 3):
        pl.when(first_z)(down[2, u].start)
    pl.when(last_z)(functools.partial(far_text, 0))
    pass_on(2, 0, 1)
    pl.when(not_last)(functools.partial(far_text, 0))
    pl.when(last_z)(functools.partial(far_text, 1))
    pass_on(2, 2, 3)
    pl.when(not_last)(functools.partial(far_text, 1))
    down_on((2, 0), (2, 1))
    pass_on(3, 0)
    down_on((2, 2), (2, 3))
    pass_on(3, 1)
    down_on((3, 0))
    pass_on(3, 2)
    down_on((3, 1))
    pass_on(3, 3)
    down_on((3, 2))
    text_rest.wait_recv()
    down_on((3, 3))
    for h in range(2):
        from_twin(h)
    coef_hops(0, 2)
    pass_on(4, 0, 1)
    down_on((4, 0), (4, 1))
    def later_hops():
        for h in range(2, 4):
            from_twin(h)
        coef_hops(2, 4)

    def first_climbs():
        climb(4, 0)
        climb(4, 1)

    pl.when(not_last)(later_hops)
    down_on((4, 2), (4, 3))
    to_twin_half[4, 0].wait_recv()
    coef_half(4, 0)
    terms_half(4, 0)
    pl.when(last_z)(later_hops)
    pl.when(last_z)(first_climbs)
    pass_on(4, 2, 3)
    terms_hops(0, 4)
    pl.when(not_last)(first_climbs)

    def text_row(r):
        at = r * MINE
        total = lax.dot_general(
            coefs[:, :, :, at : at + MINE].reshape((HOPS + 1) * 2 * ROWS, MINE),
            imgs[...].reshape((HOPS + 1) * 2 * ROWS, WIDE),
            BOTH_FIRST,
            preferred_element_type=F32,
        )
        text_sum[at : at + MINE] = total
        part_out[r] = total.astype(BF16).reshape(XS, ROWS, WIDE)

    def join(r):
        far_a[r].wait_recv()
        at = (r * XS + 1) * ROWS
        part_out[r, 1, half(0)] = (text_sum[at : at + HALF] + first_a[r].astype(F32)).astype(BF16)
        near_right[r, 0].start()
        far_b[r].wait_recv()
        at = (r * XS + 3) * ROWS + HALF
        part_out[r, 3, half(1)] = (text_sum[at : at + HALF] + first_b[r].astype(F32)).astype(BF16)
        near_left[r, 1].start()

    def row_total(r):
        near_rows[r].wait_recv()
        at = r * MINE
        return (
            text_sum[at : at + ROWS]
            + second[r, 0].astype(F32)
            + second[r, 1].astype(F32)
        )

    def join_rows():
        join(1)
        near_right[0, 1].start()
        near_left[0, 0].start()

    def image_result(c):
        rows = slice(c * HALF, (c + 1) * HALF)
        both_out[0, rows] = back_norm(img_ref[rows], inv_img[rows], grads[0, rows])

    to_twin_half[4, 1].wait_recv()
    coef_half(4, 1)
    terms_half(4, 1)
    text_row(1)
    far_a[1].start()
    far_b[1].start()
    near_right[1, 1].start()
    near_left[1, 0].start()
    climb(4, 2)
    climb(4, 3)
    text_row(0)
    far_a[0].start()
    far_b[0].start()

    def sum_row():
        row_out[...] = row_total(1).astype(BF16)
        for c in range(2):
            over[c].start()

    def own_row():
        text_sum[0:ROWS] = row_total(0)

    steps = (join_rows, functools.partial(join, 0), sum_row, own_row)

    usual = (1, 2, 3, 4)
    high = range(ZS - HOPS, ZS)
    moved = (
        {0: 0} | dict.fromkeys(high, 2),
        {0: 0, 1: 1} | dict.fromkeys(high, 3),
        {0: 1, 1: 2, 2: 2} | dict.fromkeys(high, 4),
        {0: 2, 1: 3, 2: 3, 3: 3},
    )

    def at_place(place):
        for step, common, others in zip(steps, usual, moved):
            if place == common:
                here = functools.reduce(jnp.logical_and, [z != at for at in others if others[at] != place])
                pl.when(here)(step)
            else:
                chosen = [z == at for at in others if others[at] == place]
                if chosen:
                    pl.when(functools.reduce(jnp.logical_or, chosen))(step)

    at_place(0)
    climb(3, 0)
    climb(3, 1)
    at_place(1)
    climb(3, 2)
    climb(3, 3)
    up_on((4, 3), (3, 1))
    climb(2, 0)
    climb(2, 1)
    at_place(2)
    up_on((3, 3))
    climb(2, 2)
    climb(2, 3)
    climb(1, 0)
    up_on((2, 1))
    at_place(3)
    climb(1, 2)
    climb(1, 3)
    climb(1, 1)
    climb(0, 0)
    climb(0, 2)
    climb(0, 3)
    image_result(1)
    at_place(4)
    over_all.wait_recv()
    both_out[1] = back_norm(txt_ref[...], inv_txt, text_sum[0:ROWS] + row_in[...].astype(F32))
    climb(0, 1)
    image_result(0)

    def all_left(ref, leaves):
        remote(ref, ref, twin, leaves, 0).wait_send()

    all_left(imgs, TWIN)
    all_left(txts, TEXT)
    all_left(imgs.at[0:3], PART)
    all_left(relay_down, DOWN)
    all_left(chain_out, UP)

    @pl.when(first_z)
    def _():
        all_left(relay_down, DOWN + 1)

    @pl.when(last_z)
    def _():
        all_left(relay_up, UP + 1)


N_ARRIVALS = 2 * 16 + 6 + 7 + 3 + (16 + 4) + 7


def per_device(loops, images, texts, factor, shift):
    smem = pl.BlockSpec(memory_space=pltpu.SMEM)
    hbm = pl.BlockSpec(memory_space=pltpu.HBM)
    vmem = pl.BlockSpec(memory_space=pltpu.VMEM)
    out = jax.ShapeDtypeStruct((2, ROWS, WIDE), F32)
    both = pl.pallas_call(
        functools.partial(kernel, loops),
        out_shape=out,
        in_specs=[smem, smem, hbm, hbm],
        out_specs=vmem,
        scratch_shapes=[
            pltpu.VMEM((ROWS, WIDE), BF16),
            pltpu.VMEM((ROWS, WIDE), BF16),
            pltpu.VMEM((HOPS + 1, 2, ROWS, WIDE), BF16),
            pltpu.VMEM((2, XS, ROWS, WIDE), BF16),
            pltpu.VMEM((HOPS + 1, 2, ROWS, WORDS), BF16),
            pltpu.VMEM((HOPS + 1, ROWS, WIDE), F32),
            pltpu.VMEM((WORDS, WIDE), F32),
            pltpu.VMEM((HOPS + 1, ROWS, WIDE), BF16),
            pltpu.VMEM((HOPS + 1, ROWS, WIDE), BF16),
            pltpu.VMEM((HOPS, ROWS, WIDE), BF16),
            pltpu.VMEM((HOPS, ROWS, WIDE), BF16),
            pltpu.VMEM((2, XS, ROWS, WIDE), BF16),
            pltpu.VMEM((2, HALF, WIDE), BF16),
            pltpu.VMEM((2, HALF, WIDE), BF16),
            pltpu.VMEM((2, 2, ROWS, WIDE), BF16),
            pltpu.VMEM((ROWS, WIDE), BF16),
            pltpu.VMEM((ROWS, WIDE), BF16),
            pltpu.SemaphoreType.DMA((2,)),
            pltpu.SemaphoreType.REGULAR,
            pltpu.VMEM((HOPS, ROWS, WIDE), BF16),
            pltpu.VMEM((len(ROUND), SLICE, WIDE), BF16),
            pltpu.SemaphoreType.DMA((N_LEAVES,)),
            pltpu.SemaphoreType.DMA((N_ARRIVALS,)),
        ],
        compiler_params=pltpu.CompilerParams(
            collective_id=0, has_side_effects=True, vmem_limit_bytes=48 * 2**20
        ),
        name="siglip",
    )(
        factor,
        shift,
        pltpu.with_memory_space_constraint(images, pltpu.HBM),
        pltpu.with_memory_space_constraint(texts, pltpu.HBM),
    )
    return both[0], both[1]


def solution(mesh):
    loops = mesh.shape["loop"]
    spec = P(("grp", "loop"), None)

    def step(images, texts, factor, shift):
        return per_device(loops, images, texts, factor, shift)

    return jax.shard_map(
        step, mesh=mesh, in_specs=(spec, spec, P(), P()), out_specs=(spec, spec), check_vma=False
    )
```
